256 devices in a mesh: lat: 8 (over y_lo, x), lon: 16 (over z, core), ens: 2 (over y_hi).
Axes of the slice: x: 4, y: 4 (y_hi: 2, y_lo: 2; y = y_hi * 2 + y_lo), z: 8, core: 2. Of those that a mesh axis runs over, the one named last changes fastest.
Arguments:
- grid: bfloat16 [32, 192, 2048], P(('ens', 'lat'), None, 'lon'), parts along dimension 0, may hold values from -6 to 6
- psi: bfloat16 [9, 16, 3, 2048], P(None, 'lat', None, 'lon'), may hold values from -4 to 4
- weight: bfloat16 [9, 192, 192], replicated, may hold values from -0.4375 to 0.4375
- windows: int32 [16, 2], P('lat'), may hold values from 0 to 16, as said below
- lat_rows: int32 [16, 3], P('lat'), may hold values from 0 to 15, as said below
Outputs:
- output: bfloat16 [32, 192, 2048], P(('ens', 'lat'), None, 'lon'), parts along dimension 0
The draws below stay inside these ranges and needn't reach their ends.
There are 2 independent parts, one for each index of `ens`. The reference program is written for one: setup_inputs(seed, part) draws one part's arguments, and reference() takes and returns one part's arrays. A program takes and returns all parts, laid end to end along the dimension named above; an argument that names none is the same for every part. Nothing has to cross between parts.
Inputs may be any that keep to these rules, and one draw needn't show every extreme that they name: windows[o, 0] is a block number below 16; windows[o, 1] is from 1 to 16, and latitude 0 has all 16 blocks. lat_rows[o] lists o - 1 first and o + 1 last, each clipped to the cap, and between them latitudes within 1 of o, clipped likewise.
All inputs are finite; a program needn't handle non-finite values.
Results may differ from the reference program's by a relative error of at most 0.013.
Values may be sent and summed in bfloat16 or wider, within the bound.
No kernel may reach another device: no remote copies, remote signals or barrier semaphores. Data moves between devices by JAX's collectives and lax.ppermute only.
A program may use at most 192 MiB of HBM per device.

```python
import jax
import jax.numpy as jnp
from jax import lax

C = 192
K = 9
LON_DEV = 128
HALO = 1
SPREAD = 3
NLAT = 16
LON_BLOCKS = 16
NLON = 2048


def draw_windows(key, part):
    key = jax.random.fold_in(key, 11)
    key_scale, key_shift = jax.random.split(key)
    latitude = jnp.arange(NLAT, dtype=jnp.int32)
    factor = jax.random.randint(key_scale, (NLAT,), 1, 4, dtype=jnp.int32)
    extent = jnp.clip(LON_BLOCKS * factor // (latitude + 1), 1, LON_BLOCKS)
    extent = jnp.where(latitude == 0, LON_BLOCKS, extent)
    shift = jax.random.randint(key_shift, (NLAT,), 0, 2, dtype=jnp.int32)
    first = jnp.mod(LON_BLOCKS - (extent + shift) // 2, LON_BLOCKS)
    return jnp.stack([first, extent], axis=1).astype(jnp.int32)


def draw_lat_rows(key, part):
    key = jax.random.fold_in(key, 23)
    center = jnp.arange(NLAT, dtype=jnp.int32)[:, None]
    middle = jax.random.randint(key, (NLAT, SPREAD - 2), -HALO, HALO + 1, dtype=jnp.int32)
    listed = jnp.concatenate([center - HALO, center + middle, center + HALO], axis=1)
    return jnp.clip(listed, 0, NLAT - 1).astype(jnp.int32)


def shard_levels(stream_key, shape, cuts, least, high):
    def one(dim, blocks):
        heights = jax.random.uniform(jax.random.fold_in(jax.random.fold_in(stream_key, 6), dim), (blocks,), jnp.float32, least / len(cuts), high / len(cuts))
        return jnp.repeat(jnp.exp(heights), shape[dim] // blocks).reshape((-1,) + (1,) * (len(shape) - dim - 1))

    gain = one(*cuts[0])
    for cut in cuts[1:]:
        gain = gain * one(*cut)
    return gain


def centred(own_key, dims, width, reach, cuts=(), held_as=jnp.bfloat16):
    entries = width * jax.random.normal(own_key, dims, jnp.float32)
    if cuts:
        entries = entries * shard_levels(own_key, dims, cuts, -0.22, 0.18)
    return jnp.clip(entries, -reach, reach).astype(held_as)


def setup_inputs(seed: int = 0, part: int = 0) -> dict:
    key_list = jax.random.split(jax.random.key(seed), 6)
    part_splits = jax.random.split(jax.random.fold_in(key_list[5], part), 6)
    return {
        "grid": centred(part_splits[0], (NLAT, C, NLON), 1.0, 6.0, ((0, 8), (2, 16))),
        "psi": centred(key_list[1], (K, NLAT, SPREAD, NLON), 1.0, 4.0, ((1, 8), (3, 16))),
        "weight": centred(key_list[2], (K, C, C), C ** -0.5, 0.4375),
        "windows": draw_windows(jax.random.fold_in(key_list[5], 71), part),
        "lat_rows": draw_lat_rows(jax.random.fold_in(key_list[5], 71), part),
    }


def masked_filter(full_psi, windows, block, nblocks):
    kinds, _, spread, length = full_psi.shape
    position = jnp.arange(length, dtype=jnp.int32) // block
    first = windows[:, 0]
    extent = windows[:, 1]
    inside = jnp.mod(position[None, :] - first[:, None], nblocks) < extent[:, None]
    scale = lax.rsqrt(extent.astype(jnp.float32) * float(kinds * spread * block))
    masked = full_psi.astype(jnp.float32) * jnp.where(inside, jnp.float32(1.0), jnp.float32(0.0))[None, :, None, :]
    return (masked * scale[None, :, None, None]).astype(jnp.bfloat16)

def reference(grid, psi, weight, windows, lat_rows):
    nlon = grid.shape[2]
    projected = jnp.einsum('kab,ian->kibn', weight.astype(jnp.float32), grid.astype(jnp.float32), precision=lax.Precision.HIGHEST).astype(jnp.bfloat16)
    filt = masked_filter(psi, windows, LON_DEV, LON_BLOCKS)
    filt_rows = jnp.moveaxis(filt, 1, 0)

    def one_row(items):
        rows_here, filt_here = items
        chosen = jnp.take(projected, rows_here, axis=1).astype(jnp.float32)
        spectrum = jnp.fft.rfft(chosen, axis=-1)
        kernel = jnp.conj(jnp.fft.rfft(filt_here.astype(jnp.float32), axis=-1))
        summed = lax.optimization_barrier(jnp.sum(spectrum * kernel[:, :, None, :], axis=(0, 1)))
        return jnp.fft.irfft(summed, n=nlon, axis=-1)
    result = lax.map(one_row, (lat_rows, filt_rows))
    return result.astype(jnp.bfloat16)
```

```python
import jax
import jax.numpy as jnp
from jax import lax
from jax.experimental import pallas as pl
from jax.experimental.pallas import tpu as pltpu
from jax.sharding import PartitionSpec as P

BF = jnp.bfloat16
F32 = jnp.float32
KINDS = 9
SPREAD = 3
CH = 192
BLK = 128
NB = 16
TOTAL = BLK * NB
LANES = 2 * CH
FROWS = 32
MSG = BLK + FROWS
SUB = 16


def local_filters(psi, windows, lat_rows, lat_pos, lon_pos):
    first, extent = windows[:, 0], windows[:, 1]
    inside = jnp.mod(lon_pos - first, NB) < extent
    scale = lax.rsqrt(extent.astype(F32) * float(KINDS * SPREAD * BLK))
    masked = psi.astype(F32) * jnp.where(inside, 1.0, 0.0).astype(F32)[None, :, None, None]
    filt = (masked * scale[None, :, None, None]).astype(BF).astype(F32)
    own = lat_pos * 2 + jnp.arange(2, dtype=jnp.int32)
    reach = lat_rows - own[:, None]
    by_reach = []
    for d in (-1, 0, 1):
        pick = (reach == d).astype(F32)
        by_reach.append(jnp.sum(filt * pick[None, :, :, None], axis=2).astype(BF))
    return by_reach


def conv_kernel(pos, own_ref, other_ref, w_ref, out_ref, low_ref, up_ref, xt, fv, s_ref, hs, wz):
    b = pos[0]
    z = b // 2
    c = b % 2

    deltas = (0, -1, -2, -3, 1, 2, 3, 4)
    for src, parity in ((own_ref, c), (other_ref, 1 - c)):
        for n, delta in enumerate(deltas):
            at = 2 * lax.rem(z + delta + 8, 8) + parity
            rel = lax.rem(at - b + NB, NB)
            row = pl.multiple_of(rel * BLK, BLK)
            xt[pl.ds(row, BLK), :] = src[n * MSG : n * MSG + BLK, :]
            lane = pl.multiple_of(at * BLK, BLK)
            for slot in range(3):
                fv[slot, :, pl.ds(lane, BLK)] = src[
                    n * MSG + BLK : (n + 1) * MSG, slot * BLK : (slot + 1) * BLK
                ].astype(F32)
    xt[TOTAL : TOTAL + BLK, :] = xt[0:BLK, :]

    half = CH - BLK
    wz[...] = jnp.zeros_like(wz)
    for k in range(KINDS):
        w = w_ref[k]
        wz[0, k, 0:CH, :] = w
        wz[1, k, 0:BLK, :] = w[0:BLK]
        wz[1, k, BLK + half : 2 * BLK, :] = w[BLK:CH]

    acc = []
    for i in range(2):
        for k in range(KINDS):
            for slot in range(3):
                row = fv[slot, i * KINDS + k : i * KINDS + k + 1, :]
                wide = jnp.broadcast_to(row, (SUB, TOTAL))
                skew = pltpu.roll(wide, 0, 1, stride=1, stride_axis=0)
                m = (k * 3 + slot) * SUB
                s_ref[m : m + SUB, :] = skew.astype(BF)

        @pl.loop(0, BLK // SUB)
        def _(a):
            start = pl.multiple_of(a * SUB, SUB)
            rhs = jnp.concatenate(
                [xt[pl.ds(start, TOTAL), i * BLK : (i + 1) * BLK], xt[pl.ds(start, TOTAL), 2 * BLK : 3 * BLK]],
                axis=1,
            )
            h = jnp.dot(s_ref[...], rhs, preferred_element_type=F32).astype(BF)
            for k in range(KINDS):
                for slot in range(3):
                    m = (k * 3 + slot) * SUB
                    hs[k, pl.ds(slot * BLK + start, SUB), :] = h[m : m + SUB]

        total = None
        for k in range(KINDS):
            part = lax.dot_general(wz[i, k], hs[k], (((0,), (1,)), ((), ())), preferred_element_type=F32)
            total = part if total is None else total + part
        acc.append(total)
    low_ref[...] = acc[0][:, 0:BLK].astype(BF)
    up_ref[...] = acc[1][:, 2 * BLK :].astype(BF)
    out_ref[0] = acc[0][:, BLK : 2 * BLK] + acc[1][:, 0:BLK]
    out_ref[1] = acc[0][:, 2 * BLK :] + acc[1][:, BLK : 2 * BLK]


def convolve(pos, own, other, weight):
    vmem = pl.BlockSpec(memory_space=pltpu.VMEM)
    return pl.pallas_call(
        conv_kernel,
        out_shape=(
            jax.ShapeDtypeStruct((2, CH, BLK), F32),
            jax.ShapeDtypeStruct((CH, BLK), BF),
            jax.ShapeDtypeStruct((CH, BLK), BF),
        ),
        in_specs=[pl.BlockSpec(memory_space=pltpu.SMEM), vmem, vmem, vmem],
        out_specs=(vmem, vmem, vmem),
        scratch_shapes=[
            pltpu.VMEM((TOTAL + BLK, LANES), BF),
            pltpu.VMEM((3, FROWS, TOTAL), F32),
            pltpu.VMEM((KINDS * 3 * SUB, TOTAL), BF),
            pltpu.VMEM((KINDS, 3 * BLK, 2 * BLK), BF),
            pltpu.VMEM((2, KINDS, 2 * BLK, CH), BF),
        ],
        compiler_params=pltpu.CompilerParams(vmem_limit_bytes=48 * 1024 * 1024),
    )(pos, own, other, weight)


def local(grid, psi, weight, windows, lat_rows):
    lon_pos = lax.axis_index("lon")
    lat_pos = lax.axis_index("lat")
    nlat = lax.axis_size("lat")
    up = [(j, j + 1) for j in range(nlat - 1)]
    down = [(j + 1, j) for j in range(nlat - 1)]
    below, level, above = local_filters(psi, windows, lat_rows, lat_pos, lon_pos)
    from_below = lax.ppermute(above[:, 1], "lat", up)
    from_above = lax.ppermute(below[:, 0], "lat", down)
    slots = [
        jnp.concatenate([from_below, above[:, 0]], axis=0),
        jnp.concatenate([level[:, 0], level[:, 1]], axis=0),
        jnp.concatenate([below[:, 1], from_above], axis=0),
    ]
    filters = jnp.pad(jnp.concatenate(slots, axis=1), ((0, FROWS - 2 * KINDS), (0, 0)))
    lanes = jnp.concatenate([grid[0, :BLK], grid[1, :BLK], grid[0, BLK:], grid[1, BLK:]], axis=0)
    msg = jnp.concatenate([lanes.T, filters], axis=0)

    zup = [(j, (j + 2) % NB) for j in range(NB)]
    zdown = [(j, (j - 2) % NB) for j in range(NB)]
    ups, downs = [msg], [msg]
    for _ in range(3):
        ups.append(lax.ppermute(ups[-1], "lon", zup))
        downs.append(lax.ppermute(downs[-1], "lon", zdown))
    cut = MSG // 2
    far = [
        lax.ppermute(ups[-1][:cut], "lon", zup),
        lax.ppermute(downs[-1][cut:], "lon", zdown),
    ]
    own = jnp.concatenate(ups + downs[1:] + far, axis=0)
    other = lax.ppermute(own, "lon", [(j, j ^ 1) for j in range(NB)])
    out, low, high = convolve(lon_pos.reshape(1), own, other, weight)
    to_second = lax.ppermute(low, "lat", down)
    to_first = lax.ppermute(high, "lat", up)
    return jnp.stack([out[0] + to_first.astype(F32), out[1] + to_second.astype(F32)]).astype(BF)


def solution(mesh):
    placed = (
        P(("ens", "lat"), None, "lon"),
        P(None, "lat", None, "lon"),
        P(),
        P("lat", None),
        P("lat", None),
    )
    return jax.shard_map(
        local, mesh=mesh, in_specs=placed, out_specs=P(("ens", "lat"), None, "lon"), check_vma=False
    )
```

```python
import functools

import jax
import jax.numpy as jnp
from jax import lax
from jax.experimental import pallas as pl
from jax.experimental.pallas import tpu as pltpu
from jax.sharding import PartitionSpec as P

BF = jnp.bfloat16
F16 = jnp.float16
F32 = jnp.float32
KINDS = 9
SPREAD = 3
CH = 192
BLK = 128
NB = 16
TOTAL = BLK * NB
SUB = 32
FROWS = 64
XROWS = 3 * BLK
LIFT = 2.0**13


def local_filters(psi, windows, lat_rows, lat_pos, lon_pos):
    first, extent = windows[:, 0], windows[:, 1]
    inside = jnp.mod(lon_pos - first, NB) < extent
    scale = lax.rsqrt(extent.astype(F32) * float(KINDS * SPREAD * BLK))
    masked = psi.astype(F32) * jnp.where(inside, 1.0, 0.0).astype(F32)[None, :, None, None]
    filt = (masked * scale[None, :, None, None]).astype(BF).astype(F32)
    own = lat_pos * 2 + jnp.arange(2, dtype=jnp.int32)
    reach = lat_rows - own[:, None]
    rows = []
    for o in range(2):
        for d in (-1, 0, 1):
            pick = (reach[o] == d).astype(F32)
            rows.append(jnp.sum(filt[:, o] * pick[None, :, None], axis=1))
    return jnp.concatenate(rows, axis=0).astype(BF)


def row_of(o, d):
    return (o * 3 + d + 1) * KINDS


def load_grid(xt, g_ref, b, i):
    half = CH - BLK
    for q in range(NB):
        row = pl.multiple_of(lax.rem(q - b + NB, NB) * BLK, BLK)
        xt[pl.ds(row, BLK), 0:BLK] = g_ref[q, i * BLK : (i + 1) * BLK, :]
        tail = g_ref[q, 2 * BLK : 3 * BLK, :]
        if i == 1:
            tail = jnp.concatenate([tail[:, half:], tail[:, :half]], axis=1)
        xt[pl.ds(row, BLK), BLK : 2 * BLK] = tail
    xt[TOTAL : TOTAL + BLK, :] = xt[0:BLK, :]


def correlate(xt, fv, w_ref, s_ref, hs, starts):
    count = len(starts)
    for n, at in enumerate(starts):
        for k in range(KINDS):
            row = fv[at + k : at + k + 1, :]
            wide = jnp.broadcast_to(row, (SUB, TOTAL))
            skew = pltpu.roll(wide, 0, 1, stride=1, stride_axis=0)
            m = (n * KINDS + k) * SUB
            s_ref[m : m + SUB, :] = skew.astype(BF)

    @pl.loop(0, BLK // SUB)
    def _(a):
        start = pl.multiple_of(a * SUB, SUB)
        filters = s_ref[0 : count * KINDS * SUB, :]
        h = jnp.dot(filters, xt[pl.ds(start, TOTAL), :], preferred_element_type=F32).astype(BF)
        for n in range(count):
            for k in range(KINDS):
                m = (n * KINDS + k) * SUB
                hs[k, pl.ds(pl.multiple_of(n * BLK + start, SUB), SUB), :] = h[m : m + SUB]

    total = None
    for k in range(KINDS):
        part = lax.dot_general(
            w_ref[k], hs[k, 0 : count * BLK, 0:CH], (((0,), (1,)), ((), ())), preferred_element_type=F32
        )
        total = part if total is None else total + part
    return [total[:, n * BLK : (n + 1) * BLK] for n in range(count)]


def own_kernel(i, starts, pos, g_ref, w_ref, *refs):
    *before, out_ref, xt, fv, s_ref, hs = refs
    load_grid(xt, g_ref, pos[0], i)
    for q in range(NB):
        fv[:, q * BLK : (q + 1) * BLK] = g_ref[q, XROWS : XROWS + FROWS, :].astype(F32)
    for o, part in enumerate(correlate(xt, fv, w_ref, s_ref, hs, starts)):
        out_ref[o] = part + before[0][o] if before else part


def edge_kernel(pos, g_ref, w_ref, below_ref, above_ref, low_ref, high_ref, xt, fv, s_ref, hs):
    for i, (f_ref, out_ref) in enumerate(((below_ref, low_ref), (above_ref, high_ref))):
        there = pos[1 + i] > 0

        @pl.when(there)
        def _(i=i, f_ref=f_ref, out_ref=out_ref):
            load_grid(xt, g_ref, pos[0], i)
            for q in range(NB):
                fv[:, q * BLK : (q + 1) * BLK] = f_ref[q].astype(F32)
            out_ref[...] = correlate(xt, fv, w_ref, s_ref, hs, [0])[0].astype(BF)

        @pl.when(jnp.logical_not(there))
        def _(out_ref=out_ref):
            out_ref[...] = jnp.zeros_like(out_ref)


def call(kernel, args, out_shape, pairs, frows):
    vmem = pl.BlockSpec(memory_space=pltpu.VMEM)
    return pl.pallas_call(
        kernel,
        out_shape=out_shape,
        in_specs=[pl.BlockSpec(memory_space=pltpu.SMEM)] + [vmem] * (len(args) - 1),
        out_specs=jax.tree.map(lambda _: vmem, out_shape),
        scratch_shapes=[
            pltpu.VMEM((TOTAL + BLK, 2 * BLK), BF),
            pltpu.VMEM((frows, TOTAL), F32),
            pltpu.VMEM((pairs * KINDS * SUB, TOTAL), BF),
            pltpu.VMEM((KINDS, pairs * BLK, 2 * BLK), BF),
        ],
        compiler_params=pltpu.CompilerParams(vmem_limit_bytes=40 * 1024 * 1024),
        cost_estimate=pl.CostEstimate(flops=2_000_000_000, bytes_accessed=3_000_000, transcendentals=0),
    )(*args)


def local(grid, psi, weight, windows, lat_rows):
    lon_pos = lax.axis_index("lon")
    lat_pos = lax.axis_index("lat")
    nlat = lax.axis_size("lat")
    up = [(j, (j + 1) % nlat) for j in range(nlat)]
    down = [((j + 1) % nlat, j) for j in range(nlat)]

    filters = local_filters(psi, windows, lat_rows, lat_pos, lon_pos)
    filters = jnp.pad(filters, ((0, FROWS - 6 * KINDS), (0, 0)))
    mixed = jnp.concatenate([grid[0, BLK:], grid[1, BLK:]], axis=0)
    msg = jnp.concatenate([grid[0, :BLK].T, grid[1, :BLK].T, mixed.T, filters], axis=0)
    sent = (msg.astype(F32) * LIFT).astype(F16)
    held = lax.all_gather(sent, "lon", axis=0, tiled=False)
    g = (held.astype(F32) * (1.0 / LIFT)).astype(BF)

    low_at, high_at = XROWS + row_of(0, -1), XROWS + row_of(1, 1)
    from_above = lax.ppermute(g[:, low_at : low_at + 16], "lat", down)
    from_below = lax.ppermute(g[:, high_at : high_at + 16], "lat", up)

    pos = jnp.stack([lon_pos, lat_pos, nlat - 1 - lat_pos]).astype(jnp.int32)
    halves = jax.ShapeDtypeStruct((2, CH, BLK), F32)
    edge = jax.ShapeDtypeStruct((CH, BLK), BF)
    first = call(
        functools.partial(own_kernel, 0, [row_of(0, 0), row_of(1, -1)]), (pos, g, weight), halves, 2, FROWS
    )
    low, high = call(edge_kernel, (pos, g, weight, from_below, from_above), (edge, edge), 1, 16)
    to_second = lax.ppermute(low, "lat", down)
    to_first = lax.ppermute(high, "lat", up)
    both = call(
        functools.partial(own_kernel, 1, [row_of(0, 1), row_of(1, 0)]), (pos, g, weight, first), halves, 2, FROWS
    )
    return jnp.stack([both[0] + to_first.astype(F32), both[1] + to_second.astype(F32)]).astype(BF)


def solution(mesh):
    placed = (
        P(("ens", "lat"), None, "lon"),
        P(None, "lat", None, "lon"),
        P(),
        P("lat", None),
        P("lat", None),
    )
    return jax.shard_map(
        local, mesh=mesh, in_specs=placed, out_specs=P(("ens", "lat"), None, "lon"), check_vma=False
    )
```

```python
import functools

import jax
import jax.numpy as jnp
from jax import lax
from jax.experimental import pallas as pl
from jax.experimental.pallas import tpu as pltpu
from jax.sharding import PartitionSpec as P

BF = jnp.bfloat16
F16 = jnp.float16
F32 = jnp.float32
KINDS = 9
SPREAD = 3
CH = 192
BLK = 128
NB = 16
TOTAL = BLK * NB
SUB = 32
WIDE = 64
FROWS = 64
XROWS = 3 * BLK
LIFT = 2.0**13
WIDTHS = (4, 8, 12)
WINDOW_ROW = KINDS


def row_of(o, d):
    return (o * 3 + d + 1) * KINDS + (1 if (o, d) != (0, -1) else 0)


def prepare_kernel(pos, windows, lat_rows, grid_ref, psi_ref, out_ref):
    out_ref[0:BLK] = grid_ref[0, 0:BLK].T
    out_ref[BLK : 2 * BLK] = grid_ref[1, 0:BLK].T
    mixed = jnp.concatenate([grid_ref[0, BLK:CH], grid_ref[1, BLK:CH]], axis=0)
    out_ref[2 * BLK : 3 * BLK] = mixed.T
    lane = lax.broadcasted_iota(jnp.int32, (1, BLK), 1)
    parts = []
    for o in range(2):
        first, extent = windows[o, 0], windows[o, 1]
        inside = lax.rem(pos[0] - first + NB, NB) < extent
        scale = lax.rsqrt(jnp.full((1, BLK), extent, jnp.int32).astype(F32) * float(KINDS * SPREAD * BLK))
        gate = jnp.where(inside, 1.0, 0.0).astype(F32)
        filt = [(psi_ref[:, r, o, :].astype(F32) * gate * scale).astype(BF).astype(F32) for r in range(SPREAD)]
        for d in (-1, 0, 1):
            total = jnp.zeros((KINDS, BLK), F32)
            for r in range(SPREAD):
                pick = jnp.where(lat_rows[o, r] == pos[1] * 2 + o + d, 1.0, 0.0).astype(F32)
                total = total + filt[r] * pick
            parts.append(total)
            if (o, d) in ((0, -1), (1, 1)):
                ints = jnp.where(lane == 0, first, jnp.where(lane == 1, extent, 0))
                parts.append(ints.astype(F32) * (1.0 / NB))
    parts.append(jnp.zeros((FROWS - 6 * KINDS - 2, BLK), F32))
    out_ref[XROWS : XROWS + FROWS] = jnp.concatenate(parts, axis=0).astype(BF)


def load_grid(xt, g_ref, start, i):
    half = CH - BLK
    for q in range(NB):
        row = pl.multiple_of(lax.rem(q - start + 2 * NB, NB) * BLK, BLK)
        xt[pl.ds(row, BLK), 0:BLK] = g_ref[q, i * BLK : (i + 1) * BLK, :]
        tail = g_ref[q, 2 * BLK : 3 * BLK, :]
        if i == 1:
            tail = jnp.concatenate([tail[:, half:], tail[:, :half]], axis=1)
        xt[pl.ds(row, BLK), BLK : 2 * BLK] = tail
    xt[TOTAL : TOTAL + BLK, :] = xt[0:BLK, :]


def load_filters(fv, f_ref, at, rows, start):
    for q in range(NB):
        lane = pl.multiple_of(lax.rem(q - start + NB, NB) * BLK, BLK)
        fv[0:rows, pl.ds(lane, BLK)] = f_ref[q, at : at + rows, :].astype(F32)


def correlate(xt, fv, w_ref, s_ref, hs, starts, sub, length):
    count = len(starts)
    for n, at in enumerate(starts):
        for k in range(KINDS):
            row = fv[at + k : at + k + 1, 0:length]
            wide = jnp.broadcast_to(row, (sub, length))
            skew = pltpu.roll(wide, 0, 1, stride=1, stride_axis=0)
            m = (n * KINDS + k) * sub
            s_ref[m : m + sub, 0:length] = skew.astype(BF)

    @pl.loop(0, BLK // sub)
    def _(a):
        start = pl.multiple_of(a * sub, sub)
        filters = s_ref[0 : count * KINDS * sub, 0:length]
        h = jnp.dot(filters, xt[pl.ds(start, length), :], preferred_element_type=F32).astype(BF)
        for n in range(count):
            for k in range(KINDS):
                m = (n * KINDS + k) * sub
                hs[k, pl.ds(pl.multiple_of(n * BLK + start, sub), sub), :] = h[m : m + sub]

    total = None
    for k in range(KINDS):
        part = lax.dot_general(
            w_ref[k], hs[k, 0 : count * BLK, 0:CH], (((0,), (1,)), ((), ())), preferred_element_type=F32
        )
        total = part if total is None else total + part
    return [total[:, n * BLK : (n + 1) * BLK] for n in range(count)]


def by_width(extent, widths, run):
    below = 0
    for n, width in enumerate(widths):
        last = n == len(widths) - 1

        @pl.when((extent >= below) if last else (extent >= below) & (extent < width))
        def _(width=width):
            run(width * BLK)

        below = width


def own_kernel(i, starts, pos, windows, g_ref, w_ref, *refs):
    *before, out_ref, xt, fv, s_ref, hs = refs

    def store(o, part):
        out_ref[o] = part + before[0][o] if before else part

    dense = jnp.maximum(windows[0, 1], windows[1, 1]) >= WIDTHS[-1]

    @pl.when(dense)
    def _():
        load_grid(xt, g_ref, pos[0], i)
        load_filters(fv, g_ref, XROWS, FROWS, 0)
        for o, part in enumerate(correlate(xt, fv, w_ref, s_ref, hs, starts, SUB, TOTAL)):
            store(o, part)

    @pl.when(jnp.logical_not(dense))
    def _():
        for o in range(2):
            load_grid(xt, g_ref, pos[0] + windows[o, 0], i)
            load_filters(fv, g_ref, XROWS, FROWS, windows[o, 0])
            by_width(
                windows[o, 1],
                WIDTHS,
                lambda length, o=o: store(o, correlate(xt, fv, w_ref, s_ref, hs, [starts[o]], WIDE, length)[0]),
            )


def edge_kernel(pos, g_ref, w_ref, below_ref, above_ref, low_ref, high_ref, xt, fv, s_ref, hs):
    for i, (f_ref, out_ref) in enumerate(((below_ref, low_ref), (above_ref, high_ref))):
        there = pos[1 + i] > 0

        @pl.when(there)
        def _(i=i, f_ref=f_ref, out_ref=out_ref):
            ints = (f_ref[0].astype(F32) * float(NB)).astype(jnp.int32)
            first, extent = ints[WINDOW_ROW, 0], ints[WINDOW_ROW, 1]
            load_grid(xt, g_ref, pos[0] + first, i)
            load_filters(fv, f_ref, 0, 16, first)

            def run(length):
                out_ref[...] = correlate(xt, fv, w_ref, s_ref, hs, [0], WIDE, length)[0].astype(BF)

            by_width(extent, WIDTHS + (NB,), run)

        @pl.when(jnp.logical_not(there))
        def _(out_ref=out_ref):
            out_ref[...] = jnp.zeros_like(out_ref)


def prepare(pos, windows, lat_rows, grid, psi):
    smem, vmem = pl.BlockSpec(memory_space=pltpu.SMEM), pl.BlockSpec(memory_space=pltpu.VMEM)
    return pl.pallas_call(
        prepare_kernel,
        out_shape=jax.ShapeDtypeStruct((XROWS + FROWS, BLK), BF),
        in_specs=[smem, smem, smem, vmem, vmem],
        out_specs=vmem,
    )(pos, windows, lat_rows, grid, psi)


def call(kernel, scalars, arrays, out_shape, frows):
    smem, vmem = pl.BlockSpec(memory_space=pltpu.SMEM), pl.BlockSpec(memory_space=pltpu.VMEM)
    return pl.pallas_call(
        kernel,
        out_shape=out_shape,
        in_specs=[smem] * len(scalars) + [vmem] * len(arrays),
        out_specs=jax.tree.map(lambda _: vmem, out_shape),
        scratch_shapes=[
            pltpu.VMEM((TOTAL + BLK, 2 * BLK), BF),
            pltpu.VMEM((frows, TOTAL), F32),
            pltpu.VMEM((KINDS * WIDE, TOTAL), BF),
            pltpu.VMEM((KINDS, 2 * BLK, 2 * BLK), BF),
        ],
        compiler_params=pltpu.CompilerParams(vmem_limit_bytes=40 * 1024 * 1024),
        cost_estimate=pl.CostEstimate(flops=2_000_000_000, bytes_accessed=3_000_000, transcendentals=0),
    )(*scalars, *arrays)


def local(grid, psi, weight, windows, lat_rows):
    lon_pos = lax.axis_index("lon")
    lat_pos = lax.axis_index("lat")
    nlat = lax.axis_size("lat")
    up = [(j, (j + 1) % nlat) for j in range(nlat)]
    down = [((j + 1) % nlat, j) for j in range(nlat)]
    pos = jnp.stack([lon_pos, lat_pos, nlat - 1 - lat_pos]).astype(jnp.int32)

    msg = prepare(pos, windows, lat_rows, grid, jnp.transpose(psi, (0, 2, 1, 3)))
    sent = (msg.astype(F32) * LIFT).astype(F16)
    held = lax.all_gather(sent, "lon", axis=0, tiled=False)
    g = (held.astype(F32) * (1.0 / LIFT)).astype(BF)

    low_at, high_at = XROWS + row_of(0, -1), XROWS + row_of(1, 1)
    from_above = lax.ppermute(g[:, low_at : low_at + 16], "lat", down)
    from_below = lax.ppermute(g[:, high_at : high_at + 16], "lat", up)

    halves = jax.ShapeDtypeStruct((2, CH, BLK), F32)
    edge = jax.ShapeDtypeStruct((CH, BLK), BF)
    kernel = functools.partial(own_kernel, 0, [row_of(0, 0), row_of(1, -1)])
    first = call(kernel, (pos, windows), (g, weight), halves, FROWS)
    low, high = call(edge_kernel, (pos,), (g, weight, from_below, from_above), (edge, edge), 16)
    to_second = lax.ppermute(low, "lat", down)
    to_first = lax.ppermute(high, "lat", up)
    kernel = functools.partial(own_kernel, 1, [row_of(0, 1), row_of(1, 0)])
    both = call(kernel, (pos, windows), (g, weight, first), halves, FROWS)
    return jnp.stack([both[0] + to_first.astype(F32), both[1] + to_second.astype(F32)]).astype(BF)


def solution(mesh):
    placed = (
        P(("ens", "lat"), None, "lon"),
        P(None, "lat", None, "lon"),
        P(),
        P("lat", None),
        P("lat", None),
    )
    return jax.shard_map(
        local, mesh=mesh, in_specs=placed, out_specs=P(("ens", "lat"), None, "lon"), check_vma=False
    )
```

```python
import functools

import jax
import jax.numpy as jnp
from jax import lax
from jax.experimental import pallas as pl
from jax.experimental.pallas import tpu as pltpu
from jax.sharding import PartitionSpec as P

BF = jnp.bfloat16
F16 = jnp.float16
F32 = jnp.float32
KINDS = 9
SPREAD = 3
CH = 192
BLK = 128
NB = 16
TOTAL = BLK * NB
SUB = 32
FROWS = 64
XROWS = 3 * BLK
LIFT = 2.0**13
WIDTHS = (4, 8, 12)
WINDOW_ROW = KINDS


def row_of(o, d):
    return (o * 3 + d + 1) * KINDS + (1 if (o, d) != (0, -1) else 0)


def prepare_kernel(windows, lat_rows, grid_ref, psi_ref, out_ref):
    lon, lat = lax.axis_index("lon"), lax.axis_index("lat")
    out_ref[0:BLK] = grid_ref[0, 0:BLK].T
    out_ref[BLK : 2 * BLK] = grid_ref[1, 0:BLK].T
    mixed = jnp.concatenate([grid_ref[0, BLK:CH], grid_ref[1, BLK:CH]], axis=0)
    out_ref[2 * BLK : 3 * BLK] = mixed.T
    lane = lax.broadcasted_iota(jnp.int32, (1, BLK), 1)
    parts = []
    for o in range(2):
        first, extent = windows[o, 0], windows[o, 1]
        inside = lax.rem(lon - first + NB, NB) < extent
        scale = lax.rsqrt(jnp.full((1, BLK), extent, jnp.int32).astype(F32) * float(KINDS * SPREAD * BLK))
        gate = jnp.where(inside, 1.0, 0.0).astype(F32)
        filt = [(psi_ref[:, r, o, :].astype(F32) * gate * scale).astype(BF).astype(F32) for r in range(SPREAD)]
        for d in (-1, 0, 1):
            total = jnp.zeros((KINDS, BLK), F32)
            for r in range(SPREAD):
                pick = jnp.where(lat_rows[o, r] == lat * 2 + o + d, 1.0, 0.0).astype(F32)
                total = total + filt[r] * pick
            parts.append(total)
            if (o, d) in ((0, -1), (1, 1)):
                ints = jnp.where(lane == 0, first, jnp.where(lane == 1, extent, 0))
                parts.append(ints.astype(F32) * (1.0 / NB))
    parts.append(jnp.zeros((FROWS - 6 * KINDS - 2, BLK), F32))
    out_ref[XROWS : XROWS + FROWS] = jnp.concatenate(parts, axis=0).astype(BF)


def load_grid(xt, g_ref, start, i):
    half = CH - BLK
    for q in range(NB):
        row = pl.multiple_of(lax.rem(q - start + 2 * NB, NB) * BLK, BLK)
        xt[pl.ds(row, BLK), 0:BLK] = g_ref[q, i * BLK : (i + 1) * BLK, :]
        tail = g_ref[q, 2 * BLK : 3 * BLK, :]
        if i == 1:
            tail = jnp.concatenate([tail[:, half:], tail[:, :half]], axis=1)
        xt[pl.ds(row, BLK), BLK : 2 * BLK] = tail
    xt[TOTAL : TOTAL + BLK, :] = xt[0:BLK, :]


def load_filters(fv, f_ref, at, rows, start):
    for q in range(NB):
        lane = pl.multiple_of(lax.rem(q - start + NB, NB) * BLK, BLK)
        fv[0:rows, pl.ds(lane, BLK)] = f_ref[q, at : at + rows, :].astype(F32)


def correlate(xt, fv, s_ref, hs, at, slot, length):
    base = slot * KINDS * SUB
    for k in range(KINDS):
        row = fv[at + k : at + k + 1, 0:length]
        wide = jnp.broadcast_to(row, (SUB, length))
        skew = pltpu.roll(wide, 0, 1, stride=1, stride_axis=0)
        m = base + k * SUB
        s_ref[m : m + SUB, 0:length] = skew.astype(BF)
    for start in range(0, BLK, SUB):
        filters = s_ref[base : base + KINDS * SUB, 0:length]
        h = jnp.dot(filters, xt[start : start + length, :], preferred_element_type=F32).astype(BF)
        n = slot * BLK + start
        for k in range(KINDS):
            hs[k, n : n + SUB, :] = h[k * SUB : (k + 1) * SUB]


def mix(w_ref, hs):
    total = None
    for k in range(KINDS):
        part = lax.dot_general(w_ref[k], hs[k, :, 0:CH], (((0,), (1,)), ((), ())), preferred_element_type=F32)
        total = part if total is None else total + part
    return total[:, 0:BLK], total[:, BLK : 2 * BLK]


def by_width(extent, widths, run):
    below = 0
    for n, width in enumerate(widths):
        last = n == len(widths) - 1

        @pl.when((extent >= below) if last else (extent >= below) & (extent < width))
        def _(width=width):
            run(width * BLK)

        below = width


def own_kernel(i, starts, windows, g_ref, w_ref, *refs):
    *before, out_ref, xt, fv, s_ref, hs = refs
    lon = lax.axis_index("lon")
    dense = jnp.minimum(windows[0, 1], windows[1, 1]) >= WIDTHS[-1]

    @pl.when(dense)
    def _():
        load_grid(xt, g_ref, lon, i)
        load_filters(fv, g_ref, XROWS, FROWS, 0)
        for o in range(2):
            correlate(xt, fv, s_ref, hs, starts[o], o, TOTAL)

    @pl.when(jnp.logical_not(dense))
    def _():
        for o in range(2):
            load_grid(xt, g_ref, lon + windows[o, 0], i)
            load_filters(fv, g_ref, XROWS, FROWS, windows[o, 0])
            by_width(windows[o, 1], WIDTHS + (NB,), functools.partial(correlate, xt, fv, s_ref, hs, starts[o], o))

    for o, part in enumerate(mix(w_ref, hs)):
        out_ref[o] = part + before[0][o] if before else part


def edge_kernel(g_ref, w_ref, fa_ref, fb_ref, a_ref, b_ref, xt, fv, s_ref, hs):
    lon, lat = lax.axis_index("lon"), lax.axis_index("lat")
    even = lax.rem(lat, 2) == 0
    for i in range(2):
        there = (lat > 0) if i == 0 else (lat < lax.axis_size("lat") - 1)
        take_a = jnp.logical_not(even) if i == 0 else even

        @pl.when(there)
        def _(i=i, take_a=take_a):
            got = [jnp.where(take_a, fa_ref[q].astype(F32), fb_ref[q].astype(F32)) for q in range(NB)]
            ints = (got[0] * float(NB)).astype(jnp.int32)
            first, extent = ints[WINDOW_ROW, 0], ints[WINDOW_ROW, 1]
            load_grid(xt, g_ref, lon + first, i)
            for q in range(NB):
                lane = pl.multiple_of(lax.rem(q - first + NB, NB) * BLK, BLK)
                fv[:, pl.ds(lane, BLK)] = got[q]
            by_width(extent, WIDTHS + (NB,), functools.partial(correlate, xt, fv, s_ref, hs, 0, i))

        @pl.when(jnp.logical_not(there))
        def _(i=i):
            hs[:, i * BLK : (i + 1) * BLK, :] = jnp.zeros((KINDS, BLK, 2 * BLK), BF)

    low, high = mix(w_ref, hs)
    a_ref[...] = jnp.where(even, high, low).astype(BF)
    b_ref[...] = jnp.where(even, low, high).astype(BF)


def prepare(windows, lat_rows, grid, psi):
    smem, vmem = pl.BlockSpec(memory_space=pltpu.SMEM), pl.BlockSpec(memory_space=pltpu.VMEM)
    return pl.pallas_call(
        prepare_kernel,
        out_shape=jax.ShapeDtypeStruct((XROWS + FROWS, BLK), BF),
        in_specs=[smem, smem, vmem, vmem],
        out_specs=vmem,
        compiler_params=pltpu.CompilerParams(vmem_limit_bytes=8 * 1024 * 1024),
    )(windows, lat_rows, grid, psi)


def call(kernel, scalars, arrays, out_shape, frows):
    smem, vmem = pl.BlockSpec(memory_space=pltpu.SMEM), pl.BlockSpec(memory_space=pltpu.VMEM)
    return pl.pallas_call(
        kernel,
        out_shape=out_shape,
        in_specs=[smem] * len(scalars) + [vmem] * len(arrays),
        out_specs=jax.tree.map(lambda _: vmem, out_shape),
        scratch_shapes=[
            pltpu.VMEM((TOTAL + BLK, 2 * BLK), BF),
            pltpu.VMEM((frows, TOTAL), F32),
            pltpu.VMEM((2 * KINDS * SUB, TOTAL), BF),
            pltpu.VMEM((KINDS, 2 * BLK, 2 * BLK), BF),
        ],
        compiler_params=pltpu.CompilerParams(vmem_limit_bytes=40 * 1024 * 1024),
        cost_estimate=pl.CostEstimate(flops=2_000_000_000, bytes_accessed=3_000_000, transcendentals=0),
    )(*scalars, *arrays)


def local(grid, psi, weight, windows, lat_rows):
    even = lax.rem(lax.axis_index("lat"), 2) == 0
    nlat = lax.axis_size("lat")
    pairs_a = [(j, j ^ 1) for j in range(nlat)]
    pairs_b = [(j, min(max(j - 1 + 2 * (j % 2), 0), nlat - 1)) for j in range(nlat)]

    msg = prepare(windows, lat_rows, grid, jnp.transpose(psi, (0, 2, 1, 3)))
    sent = (msg.astype(F32) * LIFT).astype(F16)
    held = lax.all_gather(sent, "lon", axis=0, tiled=False)
    g = (held.astype(F32) * (1.0 / LIFT)).astype(BF)

    low_at, high_at = XROWS + row_of(0, -1), XROWS + row_of(1, 1)
    low_filters, high_filters = g[:, low_at : low_at + 16], g[:, high_at : high_at + 16]
    filters_a = lax.ppermute(jnp.where(even, high_filters, low_filters), "lat", pairs_a)
    filters_b = lax.ppermute(jnp.where(even, low_filters, high_filters), "lat", pairs_b)

    halves = jax.ShapeDtypeStruct((2, CH, BLK), F32)
    edge = jax.ShapeDtypeStruct((CH, BLK), BF)
    kernel = functools.partial(own_kernel, 0, [row_of(0, 0), row_of(1, -1)])
    first = call(kernel, (windows,), (g, weight), halves, FROWS)
    edge_a, edge_b = call(edge_kernel, (), (g, weight, filters_a, filters_b), (edge, edge), 16)
    got_a = lax.ppermute(edge_a, "lat", pairs_a).astype(F32)
    got_b = lax.ppermute(edge_b, "lat", pairs_b).astype(F32)
    kernel = functools.partial(own_kernel, 1, [row_of(0, 1), row_of(1, 0)])
    both = call(kernel, (windows,), (g, weight, first), halves, FROWS)
    to_first, to_second = jnp.where(even, got_b, got_a), jnp.where(even, got_a, got_b)
    return jnp.stack([both[0] + to_first, both[1] + to_second]).astype(BF)


def solution(mesh):
    placed = (
        P(("ens", "lat"), None, "lon"),
        P(None, "lat", None, "lon"),
        P(),
        P("lat", None),
        P("lat", None),
    )
    return jax.shard_map(
        local, mesh=mesh, in_specs=placed, out_specs=P(("ens", "lat"), None, "lon"), check_vma=False
    )
```

```python
import functools

import jax
import jax.numpy as jnp
from jax import lax
from jax.experimental import pallas as pl
from jax.experimental.pallas import tpu as pltpu
from jax.sharding import PartitionSpec as P

BF = jnp.bfloat16
F16 = jnp.float16
F32 = jnp.float32
KINDS = 9
SPREAD = 3
CH = 192
BLK = 128
NB = 16
TOTAL = BLK * NB
SUB = 32
FROWS = 64
XROWS = 3 * BLK
LIFT = 2.0**13
WIDTHS = (4, 8, 12)
WINDOW_ROW = KINDS


def row_of(o, d):
    return (o * 3 + d + 1) * KINDS + (1 if (o, d) != (0, -1) else 0)


def prepare_kernel(windows, lat_rows, grid_ref, psi_ref, out_ref):
    lon, lat = lax.axis_index("lon"), lax.axis_index("lat")
    out_ref[0:BLK] = grid_ref[0, 0:BLK].T
    out_ref[BLK : 2 * BLK] = grid_ref[1, 0:BLK].T
    mixed = jnp.concatenate([grid_ref[0, BLK:CH], grid_ref[1, BLK:CH]], axis=0)
    out_ref[2 * BLK : 3 * BLK] = mixed.T
    lane = lax.broadcasted_iota(jnp.int32, (1, BLK), 1)
    parts = []
    for o in range(2):
        first, extent = windows[o, 0], windows[o, 1]
        inside = lax.rem(lon - first + NB, NB) < extent
        scale = lax.rsqrt(jnp.full((1, BLK), extent, jnp.int32).astype(F32) * float(KINDS * SPREAD * BLK))
        gate = jnp.where(inside, 1.0, 0.0).astype(F32)
        filt = [(psi_ref[:, r, o, :].astype(F32) * gate * scale).astype(BF).astype(F32) for r in range(SPREAD)]
        for d in (-1, 0, 1):
            total = jnp.zeros((KINDS, BLK), F32)
            for r in range(SPREAD):
                pick = jnp.where(lat_rows[o, r] == lat * 2 + o + d, 1.0, 0.0).astype(F32)
                total = total + filt[r] * pick
            parts.append(total)
            if (o, d) in ((0, -1), (1, 1)):
                ints = jnp.where(lane == 0, first, jnp.where(lane == 1, extent, 0))
                parts.append(ints.astype(F32) * (1.0 / NB))
    parts.append(jnp.zeros((FROWS - 6 * KINDS - 2, BLK), F32))
    out_ref[XROWS : XROWS + FROWS] = jnp.concatenate(parts, axis=0).astype(BF)


def load_grid(xt, g_ref, start, i):
    half = CH - BLK
    for q in range(NB):
        row = pl.multiple_of(lax.rem(q - start + 2 * NB, NB) * BLK, BLK)
        xt[pl.ds(row, BLK), 0:BLK] = g_ref[q, i * BLK : (i + 1) * BLK, :]
        tail = g_ref[q, 2 * BLK : 3 * BLK, :]
        if i == 1:
            tail = jnp.concatenate([tail[:, half:], tail[:, :half]], axis=1)
        xt[pl.ds(row, BLK), BLK : 2 * BLK] = tail
    xt[TOTAL : TOTAL + BLK, :] = xt[0:BLK, :]


def load_filters(fv, f_ref, at, rows, start):
    for q in range(NB):
        lane = pl.multiple_of(lax.rem(q - start + NB, NB) * BLK, BLK)
        fv[0:rows, pl.ds(lane, BLK)] = f_ref[q, at : at + rows, :].astype(F32)


def correlate(xt, fv, s_ref, hs, at, slot, length):
    base = slot * KINDS * SUB
    for k in range(KINDS):
        row = fv[at + k : at + k + 1, 0:length]
        wide = jnp.broadcast_to(row, (SUB, length))
        skew = pltpu.roll(wide, 0, 1, stride=1, stride_axis=0)
        m = base + k * SUB
        s_ref[m : m + SUB, 0:length] = skew.astype(BF)
    for start in range(0, BLK, SUB):
        filters = s_ref[base : base + KINDS * SUB, 0:length]
        h = jnp.dot(filters, xt[start : start + length, :], preferred_element_type=F32).astype(BF)
        n = slot * BLK + start
        for k in range(KINDS):
            hs[k, n : n + SUB, :] = h[k * SUB : (k + 1) * SUB]


def mix(w_ref, hs):
    total = None
    for k in range(KINDS):
        part = lax.dot_general(w_ref[k], hs[k, :, 0:CH], (((0,), (1,)), ((), ())), preferred_element_type=F32)
        total = part if total is None else total + part
    return total[:, 0:BLK], total[:, BLK : 2 * BLK]


def by_width(extent, widths, run):
    below = 0
    for n, width in enumerate(widths):
        last = n == len(widths) - 1

        @pl.when((extent >= below) if last else (extent >= below) & (extent < width))
        def _(width=width):
            run(width * BLK)

        below = width


def own_kernel(i, starts, windows, g_ref, w_ref, *refs):
    *before, out_ref, xt, fv, s_ref, hs = refs
    lon = lax.axis_index("lon")
    dense = jnp.minimum(windows[0, 1], windows[1, 1]) >= WIDTHS[-1]

    @pl.when(dense)
    def _():
        load_grid(xt, g_ref, lon, i)
        load_filters(fv, g_ref, XROWS, FROWS, 0)
        for o in range(2):
            correlate(xt, fv, s_ref, hs, starts[o], o, TOTAL)

    @pl.when(jnp.logical_not(dense))
    def _():
        for o in range(2):
            load_grid(xt, g_ref, lon + windows[o, 0], i)
            load_filters(fv, g_ref, XROWS, FROWS, windows[o, 0])
            by_width(windows[o, 1], WIDTHS + (NB,), functools.partial(correlate, xt, fv, s_ref, hs, starts[o], o))

    for o, part in enumerate(mix(w_ref, hs)):
        out_ref[o] = part + before[0][o] if before else part


def edge_kernel(g_ref, w_ref, below_ref, above_ref, low_ref, high_ref, xt, fv, s_ref, hs):
    lon, lat = lax.axis_index("lon"), lax.axis_index("lat")
    for i, f_ref in enumerate((below_ref, above_ref)):
        there = (lat > 0) if i == 0 else (lat < lax.axis_size("lat") - 1)

        @pl.when(there)
        def _(i=i, f_ref=f_ref):
            ints = (f_ref[0].astype(F32) * float(NB)).astype(jnp.int32)
            first, extent = ints[WINDOW_ROW, 0], ints[WINDOW_ROW, 1]
            load_grid(xt, g_ref, lon + first, i)
            load_filters(fv, f_ref, 0, 16, first)
            by_width(extent, WIDTHS + (NB,), functools.partial(correlate, xt, fv, s_ref, hs, 0, i))

        @pl.when(jnp.logical_not(there))
        def _(i=i):
            hs[:, i * BLK : (i + 1) * BLK, :] = jnp.zeros((KINDS, BLK, 2 * BLK), BF)

    low, high = mix(w_ref, hs)
    low_ref[...] = low.astype(BF)
    high_ref[...] = high.astype(BF)


def prepare(windows, lat_rows, grid, psi):
    smem, vmem = pl.BlockSpec(memory_space=pltpu.SMEM), pl.BlockSpec(memory_space=pltpu.VMEM)
    return pl.pallas_call(
        prepare_kernel,
        out_shape=jax.ShapeDtypeStruct((XROWS + FROWS, BLK), BF),
        in_specs=[smem, smem, vmem, vmem],
        out_specs=vmem,
    )(windows, lat_rows, grid, psi)


def call(kernel, scalars, arrays, out_shape, frows):
    smem, vmem = pl.BlockSpec(memory_space=pltpu.SMEM), pl.BlockSpec(memory_space=pltpu.VMEM)
    return pl.pallas_call(
        kernel,
        out_shape=out_shape,
        in_specs=[smem] * len(scalars) + [vmem] * len(arrays),
        out_specs=jax.tree.map(lambda _: vmem, out_shape),
        scratch_shapes=[
            pltpu.VMEM((TOTAL + BLK, 2 * BLK), BF),
            pltpu.VMEM((frows, TOTAL), F32),
            pltpu.VMEM((2 * KINDS * SUB, TOTAL), BF),
            pltpu.VMEM((KINDS, 2 * BLK, 2 * BLK), BF),
        ],
        compiler_params=pltpu.CompilerParams(vmem_limit_bytes=40 * 1024 * 1024),
        cost_estimate=pl.CostEstimate(flops=2_000_000_000, bytes_accessed=3_000_000, transcendentals=0),
    )(*scalars, *arrays)


def local(grid, psi, weight, windows, lat_rows):
    nlat = lax.axis_size("lat")
    up = [(j, (j + 1) % nlat) for j in range(nlat)]
    down = [((j + 1) % nlat, j) for j in range(nlat)]

    msg = prepare(windows, lat_rows, grid, jnp.transpose(psi, (0, 2, 1, 3)))
    sent = (msg.astype(F32) * LIFT).astype(F16)
    held = lax.all_gather(sent, "lon", axis=0, tiled=False)
    g = (held.astype(F32) * (1.0 / LIFT)).astype(BF)

    low_at, high_at = XROWS + row_of(0, -1), XROWS + row_of(1, 1)
    from_above = lax.ppermute(g[:, low_at : low_at + 16], "lat", down)
    from_below = lax.ppermute(g[:, high_at : high_at + 16], "lat", up)

    halves = jax.ShapeDtypeStruct((2, CH, BLK), F32)
    edge = jax.ShapeDtypeStruct((CH, BLK), BF)
    kernel = functools.partial(own_kernel, 0, [row_of(0, 0), row_of(1, -1)])
    first = call(kernel, (windows,), (g, weight), halves, FROWS)
    low, high = call(edge_kernel, (), (g, weight, from_below, from_above), (edge, edge), 16)
    to_second = lax.ppermute(low, "lat", down).astype(F32)
    to_first = lax.ppermute(high, "lat", up).astype(F32)
    kernel = functools.partial(own_kernel, 1, [row_of(0, 1), row_of(1, 0)])
    both = call(kernel, (windows,), (g, weight, first), halves, FROWS)
    return jnp.stack([both[0] + to_first, both[1] + to_second]).astype(BF)


def solution(mesh):
    placed = (
        P(("ens", "lat"), None, "lon"),
        P(None, "lat", None, "lon"),
        P(),
        P("lat", None),
        P("lat", None),
    )
    return jax.shard_map(
        local, mesh=mesh, in_specs=placed, out_specs=P(("ens", "lat"), None, "lon"), check_vma=False
    )
```

```python
import functools

import jax
import jax.numpy as jnp
from jax import lax
from jax.experimental import pallas as pl
from jax.experimental.pallas import tpu as pltpu
from jax.sharding import PartitionSpec as P

BF = jnp.bfloat16
F16 = jnp.float16
F32 = jnp.float32
KINDS = 9
SPREAD = 3
CH = 192
BLK = 128
NB = 16
TOTAL = BLK * NB
SUB = 32
FROWS = 64
XROWS = 3 * BLK
LIFT = 2.0**13
WIDTHS = (4, 8, 12)
WINDOW_ROW = KINDS


def row_of(o, d):
    return (o * 3 + d + 1) * KINDS + (1 if (o, d) != (0, -1) else 0)


def prepare_kernel(windows, lat_rows, grid_ref, psi_ref, out_ref):
    lon, lat = lax.axis_index("lon"), lax.axis_index("lat")
    out_ref[0:BLK] = grid_ref[0, 0:BLK].T
    out_ref[BLK : 2 * BLK] = grid_ref[1, 0:BLK].T
    mixed = jnp.concatenate([grid_ref[0, BLK:CH], grid_ref[1, BLK:CH]], axis=0)
    out_ref[2 * BLK : 3 * BLK] = mixed.T
    lane = lax.broadcasted_iota(jnp.int32, (1, BLK), 1)
    parts = []
    for o in range(2):
        first, extent = windows[o, 0], windows[o, 1]
        inside = lax.rem(lon - first + NB, NB) < extent
        scale = lax.rsqrt(jnp.full((1, BLK), extent, jnp.int32).astype(F32) * float(KINDS * SPREAD * BLK))
        gate = jnp.where(inside, 1.0, 0.0).astype(F32)
        filt = [(psi_ref[:, r, o, :].astype(F32) * gate * scale).astype(BF).astype(F32) for r in range(SPREAD)]
        for d in (-1, 0, 1):
            total = jnp.zeros((KINDS, BLK), F32)
            for r in range(SPREAD):
                pick = jnp.where(lat_rows[o, r] == lat * 2 + o + d, 1.0, 0.0).astype(F32)
                total = total + filt[r] * pick
            parts.append(total)
            if (o, d) in ((0, -1), (1, 1)):
                ints = jnp.where(lane == 0, first, jnp.where(lane == 1, extent, 0))
                parts.append(ints.astype(F32) * (1.0 / NB))
    parts.append(jnp.zeros((FROWS - 6 * KINDS - 2, BLK), F32))
    out_ref[XROWS : XROWS + FROWS] = jnp.concatenate(parts, axis=0).astype(BF)


def load_grid(xt, g_ref, start, i):
    half = CH - BLK
    for q in range(NB):
        row = pl.multiple_of(lax.rem(q - start + 2 * NB, NB) * BLK, BLK)
        xt[pl.ds(row, BLK), 0:BLK] = g_ref[q, i * BLK : (i + 1) * BLK, :]
        tail = g_ref[q, 2 * BLK : 3 * BLK, :]
        if i == 1:
            tail = jnp.concatenate([tail[:, half:], tail[:, :half]], axis=1)
        xt[pl.ds(row, BLK), BLK : 2 * BLK] = tail
    xt[TOTAL : TOTAL + BLK, :] = xt[0:BLK, :]


def load_filters(fv, f_ref, at, rows, start):
    for q in range(NB):
        lane = pl.multiple_of(lax.rem(q - start + NB, NB) * BLK, BLK)
        fv[0:rows, pl.ds(lane, BLK)] = f_ref[q, at : at + rows, :].astype(F32)


def correlate(xt, fv, s_ref, hs, at, slot, length):
    base = slot * KINDS * SUB
    for k in range(KINDS):
        row = fv[at + k : at + k + 1, 0:length]
        wide = jnp.broadcast_to(row, (SUB, length))
        skew = pltpu.roll(wide, 0, 1, stride=1, stride_axis=0)
        m = base + k * SUB
        s_ref[m : m + SUB, 0:length] = skew.astype(BF)
    for start in range(0, BLK, SUB):
        filters = s_ref[base : base + KINDS * SUB, 0:length]
        h = jnp.dot(filters, xt[start : start + length, :], preferred_element_type=F32).astype(BF)
        n = slot * BLK + start
        for k in range(KINDS):
            hs[k, n : n + SUB, :] = h[k * SUB : (k + 1) * SUB]


def mix(w_ref, hs):
    total = None
    for k in range(KINDS):
        part = lax.dot_general(w_ref[k], hs[k, :, 0:CH], (((0,), (1,)), ((), ())), preferred_element_type=F32)
        total = part if total is None else total + part
    return total[:, 0:BLK], total[:, BLK : 2 * BLK]


def by_width(extent, widths, run):
    below = 0
    for n, width in enumerate(widths):
        last = n == len(widths) - 1

        @pl.when((extent >= below) if last else (extent >= below) & (extent < width))
        def _(width=width):
            run(width * BLK)

        below = width


def own_kernel(i, starts, windows, g_ref, w_ref, *refs):
    *before, out_ref, xt, fv, s_ref, hs = refs
    lon = lax.axis_index("lon")
    dense = jnp.minimum(windows[0, 1], windows[1, 1]) >= WIDTHS[-1]

    @pl.when(dense)
    def _():
        load_grid(xt, g_ref, lon, i)
        load_filters(fv, g_ref, XROWS, FROWS, 0)
        for o in range(2):
            correlate(xt, fv, s_ref, hs, starts[o], o, TOTAL)

    @pl.when(jnp.logical_not(dense))
    def _():
        for o in range(2):
            load_grid(xt, g_ref, lon + windows[o, 0], i)
            load_filters(fv, g_ref, XROWS, FROWS, windows[o, 0])
            by_width(windows[o, 1], WIDTHS + (NB,), functools.partial(correlate, xt, fv, s_ref, hs, starts[o], o))

    for o, part in enumerate(mix(w_ref, hs)):
        out_ref[o] = part + before[0][o] if before else part


def edge_kernel(g_ref, w_ref, fa_ref, fb_ref, a_ref, b_ref, xt, fv, s_ref, hs):
    lon, lat = lax.axis_index("lon"), lax.axis_index("lat")
    even = lax.rem(lat, 2) == 0
    for i in range(2):
        there = (lat > 0) if i == 0 else (lat < lax.axis_size("lat") - 1)
        take_a = jnp.logical_not(even) if i == 0 else even

        @pl.when(there)
        def _(i=i, take_a=take_a):
            got = [jnp.where(take_a, fa_ref[q].astype(F32), fb_ref[q].astype(F32)) for q in range(NB)]
            ints = (got[0] * float(NB)).astype(jnp.int32)
            first, extent = ints[WINDOW_ROW, 0], ints[WINDOW_ROW, 1]
            load_grid(xt, g_ref, lon + first, i)
            for q in range(NB):
                lane = pl.multiple_of(lax.rem(q - first + NB, NB) * BLK, BLK)
                fv[:, pl.ds(lane, BLK)] = got[q]
            by_width(extent, WIDTHS + (NB,), functools.partial(correlate, xt, fv, s_ref, hs, 0, i))

        @pl.when(jnp.logical_not(there))
        def _(i=i):
            hs[:, i * BLK : (i + 1) * BLK, :] = jnp.zeros((KINDS, BLK, 2 * BLK), BF)

    low, high = mix(w_ref, hs)
    a_ref[...] = jnp.where(even, high, low).astype(BF)
    b_ref[...] = jnp.where(even, low, high).astype(BF)


def prepare(windows, lat_rows, grid, psi):
    smem, vmem = pl.BlockSpec(memory_space=pltpu.SMEM), pl.BlockSpec(memory_space=pltpu.VMEM)
    return pl.pallas_call(
        prepare_kernel,
        out_shape=jax.ShapeDtypeStruct((XROWS + FROWS, BLK), BF),
        in_specs=[smem, smem, vmem, vmem],
        out_specs=vmem,
    )(windows, lat_rows, grid, psi)


def call(kernel, scalars, arrays, out_shape, frows):
    smem, vmem = pl.BlockSpec(memory_space=pltpu.SMEM), pl.BlockSpec(memory_space=pltpu.VMEM)
    return pl.pallas_call(
        kernel,
        out_shape=out_shape,
        in_specs=[smem] * len(scalars) + [vmem] * len(arrays),
        out_specs=jax.tree.map(lambda _: vmem, out_shape),
        scratch_shapes=[
            pltpu.VMEM((TOTAL + BLK, 2 * BLK), BF),
            pltpu.VMEM((frows, TOTAL), F32),
            pltpu.VMEM((2 * KINDS * SUB, TOTAL), BF),
            pltpu.VMEM((KINDS, 2 * BLK, 2 * BLK), BF),
        ],
        compiler_params=pltpu.CompilerParams(vmem_limit_bytes=40 * 1024 * 1024),
        cost_estimate=pl.CostEstimate(flops=2_000_000_000, bytes_accessed=3_000_000, transcendentals=0),
    )(*scalars, *arrays)


def local(grid, psi, weight, windows, lat_rows):
    even = lax.rem(lax.axis_index("lat"), 2) == 0
    nlat = lax.axis_size("lat")
    pairs_a = [(j, j ^ 1) for j in range(nlat)]
    pairs_b = []
    for j in range(nlat):
        for n in range(NB):
            to = (j, n ^ 1) if j in (0, nlat - 1) else (j - 1 + 2 * (j % 2), n)
            pairs_b.append((j * NB + n, to[0] * NB + to[1]))

    msg = prepare(windows, lat_rows, grid, jnp.transpose(psi, (0, 2, 1, 3)))
    sent = (msg.astype(F32) * LIFT).astype(F16)
    held = lax.all_gather(sent, "lon", axis=0, tiled=False)
    g = (held.astype(F32) * (1.0 / LIFT)).astype(BF)

    low_at, high_at = XROWS + row_of(0, -1), XROWS + row_of(1, 1)
    low_filters, high_filters = g[:, low_at : low_at + 16], g[:, high_at : high_at + 16]
    filters_a = lax.ppermute(jnp.where(even, high_filters, low_filters), "lat", pairs_a)
    filters_b = lax.ppermute(jnp.where(even, low_filters, high_filters), ("lat", "lon"), pairs_b)

    halves = jax.ShapeDtypeStruct((2, CH, BLK), F32)
    edge = jax.ShapeDtypeStruct((CH, BLK), BF)
    kernel = functools.partial(own_kernel, 0, [row_of(0, 0), row_of(1, -1)])
    first = call(kernel, (windows,), (g, weight), halves, FROWS)
    edge_a, edge_b = call(edge_kernel, (), (g, weight, filters_a, filters_b), (edge, edge), 16)
    got_a = lax.ppermute(edge_a, "lat", pairs_a).astype(F32)
    got_b = lax.ppermute(edge_b, ("lat", "lon"), pairs_b).astype(F32)
    kernel = functools.partial(own_kernel, 1, [row_of(0, 1), row_of(1, 0)])
    both = call(kernel, (windows,), (g, weight, first), halves, FROWS)
    to_first, to_second = jnp.where(even, got_b, got_a), jnp.where(even, got_a, got_b)
    return jnp.stack([both[0] + to_first, both[1] + to_second]).astype(BF)


def solution(mesh):
    placed = (
        P(("ens", "lat"), None, "lon"),
        P(None, "lat", None, "lon"),
        P(),
        P("lat", None),
        P("lat", None),
    )
    return jax.shard_map(
        local, mesh=mesh, in_specs=placed, out_specs=P(("ens", "lat"), None, "lon"), check_vma=False
    )
```

```python
import functools

import jax
import jax.numpy as jnp
from jax import lax
from jax.experimental import pallas as pl
from jax.experimental.pallas import tpu as pltpu
from jax.sharding import PartitionSpec as P

BF = jnp.bfloat16
F16 = jnp.float16
F32 = jnp.float32
KINDS = 9
SPREAD = 3
CH = 192
BLK = 128
NB = 16
TOTAL = BLK * NB
SUB = 32
FROWS = 64
XROWS = 3 * BLK
LEVELS = 10
LIFT, STEP = 13, 12
WIDTHS = (4, 8, 12)
WINDOW_ROW = KINDS
HELD = (KINDS, 2 * BLK, 2 * BLK)


def row_of(o, d):
    return (o * 3 + d + 1) * KINDS + (1 if (o, d) != (0, -1) else 0)


def lift_of(values):
    most = jnp.max(jnp.max(jnp.abs(values), axis=0, keepdims=True), axis=1, keepdims=True)
    lift = jnp.full((1, 1), 2.0**LIFT, F32)
    level = jnp.zeros((1, 1), F32)
    for n in range(1, LEVELS):
        small = most < 2.0 ** (3 - STEP * n)
        lift = jnp.where(small, 2.0 ** (LIFT + STEP * n), lift)
        level = jnp.where(small, float(n), level)
    return lift, level


def prepare_kernel(windows, lat_rows, grid_ref, psi_ref, out_ref):
    lon, lat = lax.axis_index("lon"), lax.axis_index("lat")
    lane = lax.broadcasted_iota(jnp.int32, (1, BLK), 1)
    parts = []
    for o in range(2):
        first, extent = windows[o, 0], windows[o, 1]
        inside = lax.rem(lon - first + NB, NB) < extent
        scale = lax.rsqrt(jnp.full((1, BLK), extent, jnp.int32).astype(F32) * float(KINDS * SPREAD * BLK))
        gate = jnp.where(inside, 1.0, 0.0).astype(F32)
        filt = [(psi_ref[:, r, o, :].astype(F32) * gate * scale).astype(BF).astype(F32) for r in range(SPREAD)]
        for d in (-1, 0, 1):
            total = jnp.zeros((KINDS, BLK), F32)
            for r in range(SPREAD):
                pick = jnp.where(lat_rows[o, r] == lat * 2 + o + d, 1.0, 0.0).astype(F32)
                total = total + filt[r] * pick
            parts.append(total.astype(BF).astype(F32))
    f_lift, f_level = lift_of(jnp.concatenate(parts, axis=0))
    g_lift, g_level = lift_of(jnp.concatenate([grid_ref[0], grid_ref[1]], axis=0).astype(F32))
    parts = [part * f_lift for part in parts]
    for o, at in ((0, 1), (1, 7)):
        first, extent = windows[o, 0].astype(F32), windows[o, 1].astype(F32)
        row = jnp.where(lane == 0, first, jnp.where(lane == 1, extent, 0.0))
        row = jnp.where(lane == 2, g_level, jnp.where(lane == 3, f_level, row))
        parts.insert(at, row)
    parts.append(jnp.zeros((FROWS - 6 * KINDS - 2, BLK), F32))
    out_ref[XROWS : XROWS + FROWS] = jnp.concatenate(parts, axis=0).astype(BF)
    mixed = jnp.concatenate([grid_ref[0, BLK:CH], grid_ref[1, BLK:CH]], axis=0)
    for n, rows in enumerate((grid_ref[0, 0:BLK], grid_ref[1, 0:BLK], mixed)):
        out_ref[n * BLK : (n + 1) * BLK] = (rows.T.astype(F32) * g_lift).astype(BF)


def lower(held):
    levels = held[:, XROWS + WINDOW_ROW, 2:4].astype(F32)
    scale = jnp.full(levels.shape, 2.0**-LIFT, F32)
    for n in range(1, LEVELS):
        scale = jnp.where(levels == float(n), 2.0 ** -(LIFT + STEP * n), scale)
    row = lax.broadcasted_iota(jnp.int32, (1, XROWS + FROWS, 1), 1)
    plain = (row == XROWS + WINDOW_ROW) | (row == XROWS + row_of(1, 1) + WINDOW_ROW)
    scale = jnp.where(row < XROWS, scale[:, None, 0:1], jnp.where(plain, 1.0, scale[:, None, 1:2]))
    return (held.astype(F32) * scale).astype(BF)


def load_grid(xt, g_ref, start, i):
    half = CH - BLK
    for q in range(NB):
        row = pl.multiple_of(lax.rem(q - start + 2 * NB, NB) * BLK, BLK)
        xt[pl.ds(row, BLK), 0:BLK] = g_ref[q, i * BLK : (i + 1) * BLK, :]
        tail = g_ref[q, 2 * BLK : 3 * BLK, :]
        if i == 1:
            tail = jnp.concatenate([tail[:, half:], tail[:, :half]], axis=1)
        xt[pl.ds(row, BLK), BLK : 2 * BLK] = tail
    xt[TOTAL : TOTAL + BLK, :] = xt[0:BLK, :]


def load_filters(fv, f_ref, at, rows, start):
    for q in range(NB):
        lane = pl.multiple_of(lax.rem(q - start + NB, NB) * BLK, BLK)
        fv[0:rows, pl.ds(lane, BLK)] = f_ref[q, at : at + rows, :].astype(F32)


def correlate(xt, fv, s_ref, hs, before, at, slot, length):
    base = slot * KINDS * SUB
    for k in range(KINDS):
        row = fv[at + k : at + k + 1, 0:length]
        wide = jnp.broadcast_to(row, (SUB, length))
        skew = pltpu.roll(wide, 0, 1, stride=1, stride_axis=0)
        m = base + k * SUB
        s_ref[m : m + SUB, 0:length] = skew.astype(BF)
    for start in range(0, BLK, SUB):
        filters = s_ref[base : base + KINDS * SUB, 0:length]
        h = jnp.dot(filters, xt[start : start + length, :], preferred_element_type=F32)
        n = slot * BLK + start
        for k in range(KINDS):
            part = h[k * SUB : (k + 1) * SUB]
            if before is not None:
                part = part + before[k, n : n + SUB, :].astype(F32)
            hs[k, n : n + SUB, :] = part.astype(BF)


def mix(w_ref, hs):
    total = None
    for k in range(KINDS):
        part = lax.dot_general(w_ref[k], hs[k, :, 0:CH], (((0,), (1,)), ((), ())), preferred_element_type=F32)
        total = part if total is None else total + part
    return total[:, 0:BLK], total[:, BLK : 2 * BLK]


def by_width(extent, widths, run):
    below = 0
    for n, width in enumerate(widths):
        last = n == len(widths) - 1

        @pl.when((extent >= below) if last else (extent >= below) & (extent < width))
        def _(width=width):
            run(width * BLK)

        below = width


def correlate_own(i, starts, windows, g_ref, xt, fv, s_ref, hs, before):
    lon = lax.axis_index("lon")
    dense = jnp.minimum(windows[0, 1], windows[1, 1]) >= WIDTHS[-1]

    @pl.when(dense)
    def _():
        load_grid(xt, g_ref, lon, i)
        load_filters(fv, g_ref, XROWS, FROWS, 0)
        for o in range(2):
            correlate(xt, fv, s_ref, hs, before, starts[o], o, TOTAL)

    @pl.when(jnp.logical_not(dense))
    def _():
        for o in range(2):
            load_grid(xt, g_ref, lon + windows[o, 0], i)
            least = starts[o] // 16 * 16
            load_filters(fv, g_ref, XROWS + least, 32, windows[o, 0])
            run = functools.partial(correlate, xt, fv, s_ref, hs, before, starts[o] - least, o)
            by_width(windows[o, 1], WIDTHS + (NB,), run)


def first_kernel(windows, g_ref, hs, xt, fv, s_ref):
    correlate_own(0, (row_of(0, 0), row_of(1, -1)), windows, g_ref, xt, fv, s_ref, hs, None)


def second_kernel(windows, g_ref, w_ref, before, out_ref, xt, fv, s_ref, hs):
    correlate_own(1, (row_of(0, 1), row_of(1, 0)), windows, g_ref, xt, fv, s_ref, hs, before)
    out_ref[0], out_ref[1] = mix(w_ref, hs)


def edge_kernel(g_ref, w_ref, fa_ref, fb_ref, a_ref, b_ref, xt, fv, s_ref, hs):
    lon, lat = lax.axis_index("lon"), lax.axis_index("lat")
    even = lax.rem(lat, 2) == 0
    for i in range(2):
        there = (lat > 0) if i == 0 else (lat < lax.axis_size("lat") - 1)
        take_a = jnp.logical_not(even) if i == 0 else even

        @pl.when(there)
        def _(i=i, take_a=take_a):
            got = [jnp.where(take_a, fa_ref[q].astype(F32), fb_ref[q].astype(F32)) for q in range(NB)]
            ints = got[0].astype(jnp.int32)
            first, extent = ints[WINDOW_ROW, 0], ints[WINDOW_ROW, 1]
            load_grid(xt, g_ref, lon + first, i)
            for q in range(NB):
                lane = pl.multiple_of(lax.rem(q - first + NB, NB) * BLK, BLK)
                fv[:, pl.ds(lane, BLK)] = got[q]
            by_width(extent, WIDTHS + (NB,), functools.partial(correlate, xt, fv, s_ref, hs, None, 0, i))

        @pl.when(jnp.logical_not(there))
        def _(i=i):
            hs[:, i * BLK : (i + 1) * BLK, :] = jnp.zeros((KINDS, BLK, 2 * BLK), BF)

    low, high = mix(w_ref, hs)
    a_ref[...] = jnp.where(even, high, low).astype(BF)
    b_ref[...] = jnp.where(even, low, high).astype(BF)


def prepare(windows, lat_rows, grid, psi):
    smem, vmem = pl.BlockSpec(memory_space=pltpu.SMEM), pl.BlockSpec(memory_space=pltpu.VMEM)
    return pl.pallas_call(
        prepare_kernel,
        out_shape=jax.ShapeDtypeStruct((XROWS + FROWS, BLK), BF),
        in_specs=[smem, smem, vmem, vmem],
        out_specs=vmem,
    )(windows, lat_rows, grid, psi)


def call(kernel, scalars, arrays, out_shape, frows, keeps=True):
    smem, vmem = pl.BlockSpec(memory_space=pltpu.SMEM), pl.BlockSpec(memory_space=pltpu.VMEM)
    return pl.pallas_call(
        kernel,
        out_shape=out_shape,
        in_specs=[smem] * len(scalars) + [vmem] * len(arrays),
        out_specs=jax.tree.map(lambda _: vmem, out_shape),
        scratch_shapes=[
            pltpu.VMEM((TOTAL + BLK, 2 * BLK), BF),
            pltpu.VMEM((frows, TOTAL), F32),
            pltpu.VMEM((2 * KINDS * SUB, TOTAL), BF),
        ]
        + [pltpu.VMEM(HELD, BF)] * keeps,
        compiler_params=pltpu.CompilerParams(vmem_limit_bytes=40 * 1024 * 1024),
        cost_estimate=pl.CostEstimate(flops=2_000_000_000, bytes_accessed=3_000_000, transcendentals=0),
    )(*scalars, *arrays)


def local(grid, psi, weight, windows, lat_rows):
    even = lax.rem(lax.axis_index("lat"), 2) == 0
    nlat = lax.axis_size("lat")
    pairs_a = [(j, j ^ 1) for j in range(nlat)]
    pairs_b = []
    for j in range(nlat):
        for n in range(NB):
            to = (j, n ^ 1) if j in (0, nlat - 1) else (j - 1 + 2 * (j % 2), n)
            pairs_b.append((j * NB + n, to[0] * NB + to[1]))

    msg = prepare(windows, lat_rows, grid, jnp.transpose(psi, (0, 2, 1, 3)))
    g = lower(lax.all_gather(msg.astype(F16), "lon", axis=0, tiled=False))

    low_at, high_at = XROWS + row_of(0, -1), XROWS + row_of(1, 1)
    low_filters, high_filters = g[:, low_at : low_at + 16], g[:, high_at : high_at + 16]
    filters_a = lax.ppermute(jnp.where(even, high_filters, low_filters), "lat", pairs_a)
    filters_b = lax.ppermute(jnp.where(even, low_filters, high_filters), ("lat", "lon"), pairs_b)

    halves = jax.ShapeDtypeStruct((2, CH, BLK), F32)
    edge = jax.ShapeDtypeStruct((CH, BLK), BF)
    first = call(first_kernel, (windows,), (g,), jax.ShapeDtypeStruct(HELD, BF), FROWS, keeps=False)
    edge_a, edge_b = call(edge_kernel, (), (g, weight, filters_a, filters_b), (edge, edge), 16)
    got_a = lax.ppermute(edge_a, "lat", pairs_a).astype(F32)
    got_b = lax.ppermute(edge_b, ("lat", "lon"), pairs_b).astype(F32)
    both = call(second_kernel, (windows,), (g, weight, first), halves, FROWS)
    to_first, to_second = jnp.where(even, got_b, got_a), jnp.where(even, got_a, got_b)
    return jnp.stack([both[0] + to_first, both[1] + to_second]).astype(BF)


def solution(mesh):
    placed = (
        P(("ens", "lat"), None, "lon"),
        P(None, "lat", None, "lon"),
        P(),
        P("lat", None),
        P("lat", None),
    )
    return jax.shard_map(
        local, mesh=mesh, in_specs=placed, out_specs=P(("ens", "lat"), None, "lon"), check_vma=False
    )
```

```python
import functools

import jax
import jax.numpy as jnp
from jax import lax
from jax.experimental import pallas as pl
from jax.experimental.pallas import tpu as pltpu
from jax.sharding import PartitionSpec as P

BF = jnp.bfloat16
F16 = jnp.float16
F32 = jnp.float32
KINDS = 9
SPREAD = 3
CH = 192
BLK = 128
NB = 16
TOTAL = BLK * NB
SUB = 32
FROWS = 64
XROWS = 3 * BLK
LEVELS = 10
LIFT, STEP = 13, 12
WIDTHS = (4, 8, 12)
WINDOW_ROW = KINDS
HELD = (KINDS, 2 * BLK, 2 * BLK)


def row_of(o, d):
    return (o * 3 + d + 1) * KINDS + (1 if (o, d) != (0, -1) else 0)


def lift_of(values):
    most = jnp.max(jnp.max(jnp.abs(values), axis=0, keepdims=True), axis=1, keepdims=True)
    lift = jnp.full((1, 1), 2.0**LIFT, F32)
    level = jnp.zeros((1, 1), F32)
    for n in range(1, LEVELS):
        small = most < 2.0 ** (3 - STEP * n)
        lift = jnp.where(small, 2.0 ** (LIFT + STEP * n), lift)
        level = jnp.where(small, float(n), level)
    return lift, level


def prepare_kernel(windows, lat_rows, grid_ref, psi_ref, out_ref):
    lon, lat = lax.axis_index("lon"), lax.axis_index("lat")
    lane = lax.broadcasted_iota(jnp.int32, (1, BLK), 1)
    parts = []
    for o in range(2):
        first, extent = windows[o, 0], windows[o, 1]
        inside = lax.rem(lon - first + NB, NB) < extent
        scale = lax.rsqrt(jnp.full((1, BLK), extent, jnp.int32).astype(F32) * float(KINDS * SPREAD * BLK))
        gate = jnp.where(inside, 1.0, 0.0).astype(F32)
        filt = [(psi_ref[:, r, o, :].astype(F32) * gate * scale).astype(BF).astype(F32) for r in range(SPREAD)]
        for d in (-1, 0, 1):
            total = jnp.zeros((KINDS, BLK), F32)
            for r in range(SPREAD):
                pick = jnp.where(lat_rows[o, r] == lat * 2 + o + d, 1.0, 0.0).astype(F32)
                total = total + filt[r] * pick
            parts.append(total.astype(BF).astype(F32))
    f_lift, f_level = lift_of(jnp.concatenate(parts, axis=0))
    g_lift, g_level = lift_of(jnp.concatenate([grid_ref[0], grid_ref[1]], axis=0).astype(F32))
    parts = [part * f_lift for part in parts]
    for o, at in ((0, 1), (1, 7)):
        first, extent = windows[o, 0].astype(F32), windows[o, 1].astype(F32)
        row = jnp.where(lane == 0, first, jnp.where(lane == 1, extent, 0.0))
        row = jnp.where(lane == 2, g_level, jnp.where(lane == 3, f_level, row))
        parts.insert(at, row * (2.0**LIFT / NB))
    parts.append(jnp.zeros((FROWS - 6 * KINDS - 2, BLK), F32))
    out_ref[XROWS : XROWS + FROWS] = jnp.concatenate(parts, axis=0).astype(BF)
    mixed = jnp.concatenate([grid_ref[0, BLK:CH], grid_ref[1, BLK:CH]], axis=0)
    for n, rows in enumerate((grid_ref[0, 0:BLK], grid_ref[1, 0:BLK], mixed)):
        out_ref[n * BLK : (n + 1) * BLK] = (rows.T.astype(F32) * g_lift).astype(BF)


def window_row(ref, q, at):
    return ref[q, at : at + 16, :].astype(F32)[WINDOW_ROW : WINDOW_ROW + 1]


def any_level(ref, at):
    rows = window_row(ref, 0, at)
    for q in range(1, NB):
        rows = jnp.maximum(rows, window_row(ref, q, at))
    lane = lax.broadcasted_iota(jnp.int32, rows.shape, 1)
    return jnp.max(jnp.where((lane == 2) | (lane == 3), rows, 0.0)) > 0


def lower(ref, q, at, lane):
    level = window_row(ref, q, at)[:, lane : lane + 1] * float(NB)
    scale = jnp.full((1, 1), 1.0, F32)
    for n in range(1, LEVELS):
        scale = jnp.where(level == float(n), 2.0 ** (-STEP * n), scale)
    return scale


def load_grid(xt, g_ref, start, i, lifted):
    half = CH - BLK

    def row_of_block(q):
        return pl.multiple_of(lax.rem(q - start + 2 * NB, NB) * BLK, BLK)

    for q in range(NB):
        row = row_of_block(q)
        xt[pl.ds(row, BLK), 0:BLK] = g_ref[q, i * BLK : (i + 1) * BLK, :]
        tail = g_ref[q, 2 * BLK : 3 * BLK, :]
        if i == 1:
            tail = jnp.concatenate([tail[:, half:], tail[:, :half]], axis=1)
        xt[pl.ds(row, BLK), BLK : 2 * BLK] = tail

    @pl.when(lifted)
    def _():
        @pl.loop(0, NB)
        def _(q):
            rows = pl.ds(row_of_block(q), BLK)
            xt[rows, :] = (xt[rows, :].astype(F32) * lower(g_ref, q, XROWS, 2)).astype(BF)

    xt[TOTAL : TOTAL + BLK, :] = xt[0:BLK, :]


def load_filters(fv, f_ref, at, rows, start, lifted, info):
    def lanes_of_block(q):
        return pl.ds(pl.multiple_of(lax.rem(q - start + NB, NB) * BLK, BLK), BLK)

    for q in range(NB):
        fv[0:rows, lanes_of_block(q)] = f_ref[q, at : at + rows, :].astype(F32)

    @pl.when(lifted)
    def _():
        @pl.loop(0, NB)
        def _(q):
            lanes = lanes_of_block(q)
            fv[0:rows, lanes] = fv[0:rows, lanes] * lower(f_ref, q, info, 3)


def correlate(xt, fv, s_ref, hs, before, at, slot, length):
    base = slot * KINDS * SUB
    for k in range(KINDS):
        row = fv[at + k : at + k + 1, 0:length]
        wide = jnp.broadcast_to(row, (SUB, length))
        skew = pltpu.roll(wide, 0, 1, stride=1, stride_axis=0)
        m = base + k * SUB
        s_ref[m : m + SUB, 0:length] = skew.astype(BF)
    for start in range(0, BLK, SUB):
        filters = s_ref[base : base + KINDS * SUB, 0:length]
        h = jnp.dot(filters, xt[start : start + length, :], preferred_element_type=F32)
        n = slot * BLK + start
        for k in range(KINDS):
            part = h[k * SUB : (k + 1) * SUB]
            if before is not None:
                part = part + before[k, n : n + SUB, :].astype(F32)
            hs[k, n : n + SUB, :] = part.astype(BF)


def mix(w_ref, hs):
    total = None
    for k in range(KINDS):
        part = lax.dot_general(w_ref[k], hs[k, :, 0:CH], (((0,), (1,)), ((), ())), preferred_element_type=F32)
        total = part if total is None else total + part
    return total[:, 0:BLK], total[:, BLK : 2 * BLK]


def by_width(extent, widths, run):
    below = 0
    for n, width in enumerate(widths):
        last = n == len(widths) - 1

        @pl.when((extent >= below) if last else (extent >= below) & (extent < width))
        def _(width=width):
            run(width * BLK)

        below = width


def correlate_own(i, starts, windows, g_ref, xt, fv, s_ref, hs, before):
    lon = lax.axis_index("lon")
    lifted = any_level(g_ref, XROWS)
    dense = jnp.minimum(windows[0, 1], windows[1, 1]) >= WIDTHS[-1]

    @pl.when(dense)
    def _():
        load_grid(xt, g_ref, lon, i, lifted)
        load_filters(fv, g_ref, XROWS, FROWS, 0, lifted, XROWS)
        for o in range(2):
            correlate(xt, fv, s_ref, hs, before, starts[o], o, TOTAL)

    @pl.when(jnp.logical_not(dense))
    def _():
        for o in range(2):
            load_grid(xt, g_ref, lon + windows[o, 0], i, lifted)
            least = starts[o] // 16 * 16
            load_filters(fv, g_ref, XROWS + least, 32, windows[o, 0], lifted, XROWS)
            run = functools.partial(correlate, xt, fv, s_ref, hs, before, starts[o] - least, o)
            by_width(windows[o, 1], WIDTHS + (NB,), run)


def first_kernel(windows, g_ref, hs, xt, fv, s_ref):
    correlate_own(0, (row_of(0, 0), row_of(1, -1)), windows, g_ref, xt, fv, s_ref, hs, None)


def second_kernel(windows, g_ref, w_ref, before, out_ref, xt, fv, s_ref, hs):
    correlate_own(1, (row_of(0, 1), row_of(1, 0)), windows, g_ref, xt, fv, s_ref, hs, before)
    out_ref[0], out_ref[1] = mix(w_ref, hs)


def edge_kernel(g_ref, w_ref, fa_ref, fb_ref, a_ref, b_ref, xt, fv, s_ref, got, hs):
    lon, lat = lax.axis_index("lon"), lax.axis_index("lat")
    even = lax.rem(lat, 2) == 0
    grid_lifted = any_level(g_ref, XROWS)
    for i in range(2):
        there = (lat > 0) if i == 0 else (lat < lax.axis_size("lat") - 1)
        take_a = jnp.logical_not(even) if i == 0 else even

        @pl.when(there)
        def _(i=i, take_a=take_a):
            for q in range(NB):
                got[q] = jnp.where(take_a, fa_ref[q].astype(F32), fb_ref[q].astype(F32)).astype(BF)
            ints = (got[0].astype(F32) * float(NB)).astype(jnp.int32)
            first, extent = ints[WINDOW_ROW, 0], ints[WINDOW_ROW, 1]
            load_grid(xt, g_ref, lon + first, i, grid_lifted)
            load_filters(fv, got, 0, 16, first, any_level(got, 0), 0)
            by_width(extent, WIDTHS + (NB,), functools.partial(correlate, xt, fv, s_ref, hs, None, 0, i))

        @pl.when(jnp.logical_not(there))
        def _(i=i):
            hs[:, i * BLK : (i + 1) * BLK, :] = jnp.zeros((KINDS, BLK, 2 * BLK), BF)

    low, high = mix(w_ref, hs)
    a_ref[...] = jnp.where(even, high, low).astype(BF)
    b_ref[...] = jnp.where(even, low, high).astype(BF)


def prepare(windows, lat_rows, grid, psi):
    smem, vmem = pl.BlockSpec(memory_space=pltpu.SMEM), pl.BlockSpec(memory_space=pltpu.VMEM)
    return pl.pallas_call(
        prepare_kernel,
        out_shape=jax.ShapeDtypeStruct((XROWS + FROWS, BLK), BF),
        in_specs=[smem, smem, vmem, vmem],
        out_specs=vmem,
    )(windows, lat_rows, grid, psi)


def call(kernel, scalars, arrays, out_shape, frows, more=(HELD,)):
    smem, vmem = pl.BlockSpec(memory_space=pltpu.SMEM), pl.BlockSpec(memory_space=pltpu.VMEM)
    return pl.pallas_call(
        kernel,
        out_shape=out_shape,
        in_specs=[smem] * len(scalars) + [vmem] * len(arrays),
        out_specs=jax.tree.map(lambda _: vmem, out_shape),
        scratch_shapes=[
            pltpu.VMEM((TOTAL + BLK, 2 * BLK), BF),
            pltpu.VMEM((frows, TOTAL), F32),
            pltpu.VMEM((2 * KINDS * SUB, TOTAL), BF),
        ]
        + [pltpu.VMEM(shape, BF) for shape in more],
        compiler_params=pltpu.CompilerParams(vmem_limit_bytes=40 * 1024 * 1024),
        cost_estimate=pl.CostEstimate(flops=2_000_000_000, bytes_accessed=3_000_000, transcendentals=0),
    )(*scalars, *arrays)


def local(grid, psi, weight, windows, lat_rows):
    even = lax.rem(lax.axis_index("lat"), 2) == 0
    nlat = lax.axis_size("lat")
    pairs_a = [(j, j ^ 1) for j in range(nlat)]
    pairs_b = []
    for j in range(nlat):
        for n in range(NB):
            to = (j, n ^ 1) if j in (0, nlat - 1) else (j - 1 + 2 * (j % 2), n)
            pairs_b.append((j * NB + n, to[0] * NB + to[1]))

    msg = prepare(windows, lat_rows, grid, jnp.transpose(psi, (0, 2, 1, 3)))
    held = lax.all_gather(msg.astype(F16), "lon", axis=0, tiled=False)
    g = (held.astype(F32) * 2.0**-LIFT).astype(BF)

    low_at, high_at = XROWS + row_of(0, -1), XROWS + row_of(1, 1)
    low_filters, high_filters = g[:, low_at : low_at + 16], g[:, high_at : high_at + 16]
    filters_a = lax.ppermute(jnp.where(even, high_filters, low_filters), "lat", pairs_a)
    filters_b = lax.ppermute(jnp.where(even, low_filters, high_filters), ("lat", "lon"), pairs_b)

    halves = jax.ShapeDtypeStruct((2, CH, BLK), F32)
    edge = jax.ShapeDtypeStruct((CH, BLK), BF)
    first = call(first_kernel, (windows,), (g,), jax.ShapeDtypeStruct(HELD, BF), FROWS, more=())
    edge_a, edge_b = call(edge_kernel, (), (g, weight, filters_a, filters_b), (edge, edge), 16, ((NB, 16, BLK), HELD))
    got_a = lax.ppermute(edge_a, "lat", pairs_a).astype(F32)
    got_b = lax.ppermute(edge_b, ("lat", "lon"), pairs_b).astype(F32)
    both = call(second_kernel, (windows,), (g, weight, first), halves, FROWS)
    to_first, to_second = jnp.where(even, got_b, got_a), jnp.where(even, got_a, got_b)
    return jnp.stack([both[0] + to_first, both[1] + to_second]).astype(BF)


def solution(mesh):
    placed = (
        P(("ens", "lat"), None, "lon"),
        P(None, "lat", None, "lon"),
        P(),
        P("lat", None),
        P("lat", None),
    )
    return jax.shard_map(
        local, mesh=mesh, in_specs=placed, out_specs=P(("ens", "lat"), None, "lon"), check_vma=False
    )
```

```python
import functools

import jax
import jax.numpy as jnp
from jax import lax
from jax.experimental import pallas as pl
from jax.experimental.pallas import tpu as pltpu
from jax.sharding import PartitionSpec as P

BF = jnp.bfloat16
F16 = jnp.float16
F32 = jnp.float32
KINDS = 9
SPREAD = 3
CH = 192
BLK = 128
NB = 16
TOTAL = BLK * NB
SUB = 32
FROWS = 64
XROWS = 3 * BLK
LEVELS = 10
LIFT, STEP = 13, 12
WIDTHS = (4, 8, 12)
WINDOW_ROW = KINDS
HELD = (KINDS, 2 * BLK, 2 * BLK)


def row_of(o, d):
    return (o * 3 + d + 1) * KINDS + (1 if (o, d) != (0, -1) else 0)


def lift_of(values):
    most = jnp.max(jnp.max(jnp.abs(values), axis=0, keepdims=True), axis=1, keepdims=True)
    lift = jnp.full((1, 1), 2.0**LIFT, F32)
    level = jnp.zeros((1, 1), F32)
    for n in range(1, LEVELS):
        small = (most < 2.0 ** (3 - STEP * n)) & (most > 0.0)
        lift = jnp.where(small, 2.0 ** (LIFT + STEP * n), lift)
        level = jnp.where(small, float(n), level)
    return lift, level


def prepare_kernel(windows, lat_rows, grid_ref, psi_ref, out_ref):
    lon, lat = lax.axis_index("lon"), lax.axis_index("lat")
    lane = lax.broadcasted_iota(jnp.int32, (1, BLK), 1)
    parts = []
    for o in range(2):
        first, extent = windows[o, 0], windows[o, 1]
        inside = lax.rem(lon - first + NB, NB) < extent
        scale = lax.rsqrt(jnp.full((1, BLK), extent, jnp.int32).astype(F32) * float(KINDS * SPREAD * BLK))
        gate = jnp.where(inside, 1.0, 0.0).astype(F32)
        filt = [(psi_ref[:, r, o, :].astype(F32) * gate * scale).astype(BF).astype(F32) for r in range(SPREAD)]
        for d in (-1, 0, 1):
            total = jnp.zeros((KINDS, BLK), F32)
            for r in range(SPREAD):
                pick = jnp.where(lat_rows[o, r] == lat * 2 + o + d, 1.0, 0.0).astype(F32)
                total = total + filt[r] * pick
            parts.append(total.astype(BF).astype(F32))
    f_lift, f_level = lift_of(jnp.concatenate(parts, axis=0))
    g_lift, g_level = lift_of(jnp.concatenate([grid_ref[0], grid_ref[1]], axis=0).astype(F32))
    parts = [part * f_lift for part in parts]
    for o, at in ((0, 1), (1, 7)):
        first, extent = windows[o, 0].astype(F32), windows[o, 1].astype(F32)
        row = jnp.where(lane == 0, first, jnp.where(lane == 1, extent, 0.0))
        row = jnp.where(lane == 2, g_level, jnp.where(lane == 3, f_level, row))
        parts.insert(at, row * (2.0**LIFT / NB))
    parts.append(jnp.zeros((FROWS - 6 * KINDS - 2, BLK), F32))
    out_ref[XROWS : XROWS + FROWS] = jnp.concatenate(parts, axis=0).astype(BF)
    mixed = jnp.concatenate([grid_ref[0, BLK:CH], grid_ref[1, BLK:CH]], axis=0)
    for n, rows in enumerate((grid_ref[0, 0:BLK], grid_ref[1, 0:BLK], mixed)):
        out_ref[n * BLK : (n + 1) * BLK] = (rows.T.astype(F32) * g_lift).astype(BF)


def window_row(ref, q, at):
    return ref[q, at : at + 16, :].astype(F32)[WINDOW_ROW : WINDOW_ROW + 1]


def any_level(ref, at):
    rows = window_row(ref, 0, at)
    for q in range(1, NB):
        rows = jnp.maximum(rows, window_row(ref, q, at))
    lane = lax.broadcasted_iota(jnp.int32, rows.shape, 1)
    return jnp.max(jnp.where((lane == 2) | (lane == 3), rows, 0.0)) > 0


def lower(ref, q, at, lane):
    level = window_row(ref, q, at)[:, lane : lane + 1] * float(NB)
    scale = jnp.full((1, 1), 1.0, F32)
    for n in range(1, LEVELS):
        scale = jnp.where(level == float(n), 2.0 ** (-STEP * n), scale)
    return scale


def load_grid(xt, g_ref, start, i, lifted):
    half = CH - BLK

    def row_of_block(q):
        return pl.multiple_of(lax.rem(q - start + 2 * NB, NB) * BLK, BLK)

    for q in range(NB):
        row = row_of_block(q)
        xt[pl.ds(row, BLK), 0:BLK] = g_ref[q, i * BLK : (i + 1) * BLK, :]
        tail = g_ref[q, 2 * BLK : 3 * BLK, :]
        if i == 1:
            tail = jnp.concatenate([tail[:, half:], tail[:, :half]], axis=1)
        xt[pl.ds(row, BLK), BLK : 2 * BLK] = tail

    @pl.when(lifted)
    def _():
        @pl.loop(0, NB)
        def _(q):
            rows = pl.ds(row_of_block(q), BLK)
            xt[rows, :] = (xt[rows, :].astype(F32) * lower(g_ref, q, XROWS, 2)).astype(BF)

    xt[TOTAL : TOTAL + BLK, :] = xt[0:BLK, :]


def load_filters(fv, f_ref, at, rows, start, lifted, info):
    def lanes_of_block(q):
        return pl.ds(pl.multiple_of(lax.rem(q - start + NB, NB) * BLK, BLK), BLK)

    for q in range(NB):
        fv[0:rows, lanes_of_block(q)] = f_ref[q, at : at + rows, :].astype(F32)

    @pl.when(lifted)
    def _():
        @pl.loop(0, NB)
        def _(q):
            lanes = lanes_of_block(q)
            fv[0:rows, lanes] = fv[0:rows, lanes] * lower(f_ref, q, info, 3)


def correlate(xt, fv, s_ref, hs, before, at, slot, length):
    base = slot * KINDS * SUB
    for k in range(KINDS):
        row = fv[at + k : at + k + 1, 0:length]
        wide = jnp.broadcast_to(row, (SUB, length))
        skew = pltpu.roll(wide, 0, 1, stride=1, stride_axis=0)
        m = base + k * SUB
        s_ref[m : m + SUB, 0:length] = skew.astype(BF)
    for start in range(0, BLK, SUB):
        filters = s_ref[base : base + KINDS * SUB, 0:length]
        h = jnp.dot(filters, xt[start : start + length, :], preferred_element_type=F32)
        n = slot * BLK + start
        for k in range(KINDS):
            part = h[k * SUB : (k + 1) * SUB]
            if before is not None:
                part = part + before[k, n : n + SUB, :].astype(F32)
            hs[k, n : n + SUB, :] = part.astype(BF)


def mix(w_ref, hs):
    total = None
    for k in range(KINDS):
        part = lax.dot_general(w_ref[k], hs[k, :, 0:CH], (((0,), (1,)), ((), ())), preferred_element_type=F32)
        total = part if total is None else total + part
    return total[:, 0:BLK], total[:, BLK : 2 * BLK]


def by_width(extent, widths, run):
    below = 0
    for n, width in enumerate(widths):
        last = n == len(widths) - 1

        @pl.when((extent >= below) if last else (extent >= below) & (extent < width))
        def _(width=width):
            run(width * BLK)

        below = width


def correlate_own(i, starts, windows, g_ref, xt, fv, s_ref, hs, before):
    lon = lax.axis_index("lon")
    lifted = any_level(g_ref, XROWS)
    dense = jnp.minimum(windows[0, 1], windows[1, 1]) >= WIDTHS[-1]

    @pl.when(dense)
    def _():
        load_grid(xt, g_ref, lon, i, lifted)
        load_filters(fv, g_ref, XROWS, FROWS, 0, lifted, XROWS)
        for o in range(2):
            correlate(xt, fv, s_ref, hs, before, starts[o], o, TOTAL)

    @pl.when(jnp.logical_not(dense))
    def _():
        for o in range(2):
            load_grid(xt, g_ref, lon + windows[o, 0], i, lifted)
            least = starts[o] // 16 * 16
            load_filters(fv, g_ref, XROWS + least, 32, windows[o, 0], lifted, XROWS)
            run = functools.partial(correlate, xt, fv, s_ref, hs, before, starts[o] - least, o)
            by_width(windows[o, 1], WIDTHS + (NB,), run)


def first_kernel(windows, g_ref, hs, xt, fv, s_ref):
    correlate_own(0, (row_of(0, 0), row_of(1, -1)), windows, g_ref, xt, fv, s_ref, hs, None)


def second_kernel(windows, g_ref, w_ref, before, out_ref, xt, fv, s_ref, hs):
    correlate_own(1, (row_of(0, 1), row_of(1, 0)), windows, g_ref, xt, fv, s_ref, hs, before)
    out_ref[0], out_ref[1] = mix(w_ref, hs)


def edge_kernel(g_ref, w_ref, fa_ref, fb_ref, a_ref, b_ref, xt, fv, s_ref, got, hs):
    lon, lat = lax.axis_index("lon"), lax.axis_index("lat")
    even = lax.rem(lat, 2) == 0
    grid_lifted = any_level(g_ref, XROWS)
    for i in range(2):
        there = (lat > 0) if i == 0 else (lat < lax.axis_size("lat") - 1)
        take_a = jnp.logical_not(even) if i == 0 else even

        @pl.when(there)
        def _(i=i, take_a=take_a):
            for q in range(NB):
                got[q] = jnp.where(take_a, fa_ref[q].astype(F32), fb_ref[q].astype(F32)).astype(BF)
            ints = (got[0].astype(F32) * float(NB)).astype(jnp.int32)
            first, extent = ints[WINDOW_ROW, 0], ints[WINDOW_ROW, 1]
            load_grid(xt, g_ref, lon + first, i, grid_lifted)
            load_filters(fv, got, 0, 16, first, any_level(got, 0), 0)
            by_width(extent, WIDTHS + (NB,), functools.partial(correlate, xt, fv, s_ref, hs, None, 0, i))

        @pl.when(jnp.logical_not(there))
        def _(i=i):
            hs[:, i * BLK : (i + 1) * BLK, :] = jnp.zeros((KINDS, BLK, 2 * BLK), BF)

    low, high = mix(w_ref, hs)
    a_ref[...] = jnp.where(even, high, low).astype(BF)
    b_ref[...] = jnp.where(even, low, high).astype(BF)


def prepare(windows, lat_rows, grid, psi):
    smem, vmem = pl.BlockSpec(memory_space=pltpu.SMEM), pl.BlockSpec(memory_space=pltpu.VMEM)
    return pl.pallas_call(
        prepare_kernel,
        out_shape=jax.ShapeDtypeStruct((XROWS + FROWS, BLK), BF),
        in_specs=[smem, smem, vmem, vmem],
        out_specs=vmem,
    )(windows, lat_rows, grid, psi)


def call(kernel, scalars, arrays, out_shape, frows, more=(HELD,)):
    smem, vmem = pl.BlockSpec(memory_space=pltpu.SMEM), pl.BlockSpec(memory_space=pltpu.VMEM)
    return pl.pallas_call(
        kernel,
        out_shape=out_shape,
        in_specs=[smem] * len(scalars) + [vmem] * len(arrays),
        out_specs=jax.tree.map(lambda _: vmem, out_shape),
        scratch_shapes=[
            pltpu.VMEM((TOTAL + BLK, 2 * BLK), BF),
            pltpu.VMEM((frows, TOTAL), F32),
            pltpu.VMEM((2 * KINDS * SUB, TOTAL), BF),
        ]
        + [pltpu.VMEM(shape, BF) for shape in more],
        compiler_params=pltpu.CompilerParams(vmem_limit_bytes=40 * 1024 * 1024),
        cost_estimate=pl.CostEstimate(flops=2_000_000_000, bytes_accessed=3_000_000, transcendentals=0),
    )(*scalars, *arrays)


def local(grid, psi, weight, windows, lat_rows):
    even = lax.rem(lax.axis_index("lat"), 2) == 0
    nlat = lax.axis_size("lat")
    pairs_a = [(j, j ^ 1) for j in range(nlat)]
    pairs_b = []
    for j in range(nlat):
        for n in range(NB):
            to = (j, n ^ 1) if j in (0, nlat - 1) else (j - 1 + 2 * (j % 2), n)
            pairs_b.append((j * NB + n, to[0] * NB + to[1]))

    msg = prepare(windows, lat_rows, grid, jnp.transpose(psi, (0, 2, 1, 3)))
    held = lax.all_gather(msg.astype(F16), "lon", axis=0, tiled=False)
    g = (held.astype(F32) * 2.0**-LIFT).astype(BF)

    low_at, high_at = XROWS + row_of(0, -1), XROWS + row_of(1, 1)
    low_filters, high_filters = g[:, low_at : low_at + 16], g[:, high_at : high_at + 16]
    filters_a = lax.ppermute(jnp.where(even, high_filters, low_filters), "lat", pairs_a)
    filters_b = lax.ppermute(jnp.where(even, low_filters, high_filters), ("lat", "lon"), pairs_b)

    halves = jax.ShapeDtypeStruct((2, CH, BLK), F32)
    edge = jax.ShapeDtypeStruct((CH, BLK), BF)
    first = call(first_kernel, (windows,), (g,), jax.ShapeDtypeStruct(HELD, BF), FROWS, more=())
    edge_a, edge_b = call(edge_kernel, (), (g, weight, filters_a, filters_b), (edge, edge), 16, ((NB, 16, BLK), HELD))
    got_a = lax.ppermute(edge_a, "lat", pairs_a).astype(F32)
    got_b = lax.ppermute(edge_b, ("lat", "lon"), pairs_b).astype(F32)
    both = call(second_kernel, (windows,), (g, weight, first), halves, FROWS)
    to_first, to_second = jnp.where(even, got_b, got_a), jnp.where(even, got_a, got_b)
    return jnp.stack([both[0] + to_first, both[1] + to_second]).astype(BF)


def solution(mesh):
    placed = (
        P(("ens", "lat"), None, "lon"),
        P(None, "lat", None, "lon"),
        P(),
        P("lat", None),
        P("lat", None),
    )
    return jax.shard_map(
        local, mesh=mesh, in_specs=placed, out_specs=P(("ens", "lat"), None, "lon"), check_vma=False
    )
```

```python
import functools

import jax
import jax.numpy as jnp
from jax import lax
from jax.experimental import pallas as pl
from jax.experimental.pallas import tpu as pltpu
from jax.sharding import PartitionSpec as P

BF = jnp.bfloat16
F16 = jnp.float16
F32 = jnp.float32
KINDS = 9
SPREAD = 3
CH = 192
BLK = 128
NB = 16
TOTAL = BLK * NB
SUB = 32
FROWS = 64
XROWS = 3 * BLK
LEVELS = 10
LIFT, STEP = 13, 12
WIDTHS = (4, 8, 12)
WINDOW_ROW = KINDS
HELD = (KINDS, 2 * BLK, 2 * BLK)


def row_of(o, d):
    return (o * 3 + d + 1) * KINDS + (1 if (o, d) != (0, -1) else 0)


def lift_of(values):
    most = jnp.max(jnp.max(jnp.abs(values), axis=0, keepdims=True), axis=1, keepdims=True)
    lift = jnp.full((1, 1), 2.0**LIFT, F32)
    level = jnp.zeros((1, 1), F32)
    for n in range(1, LEVELS):
        small = (most < 2.0 ** (3 - STEP * n)) & (most > 0.0)
        lift = jnp.where(small, 2.0 ** (LIFT + STEP * n), lift)
        level = jnp.where(small, float(n), level)
    return lift, level


def prepare_kernel(windows, lat_rows, grid_ref, psi_ref, out_ref):
    lon, lat = lax.axis_index("lon"), lax.axis_index("lat")
    lane = lax.broadcasted_iota(jnp.int32, (1, BLK), 1)
    parts = []
    for o in range(2):
        first, extent = windows[o, 0], windows[o, 1]
        inside = lax.rem(lon - first + NB, NB) < extent
        scale = lax.rsqrt(jnp.full((1, BLK), extent, jnp.int32).astype(F32) * float(KINDS * SPREAD * BLK))
        gate = jnp.where(inside, 1.0, 0.0).astype(F32)
        filt = [(psi_ref[:, r, o, :].astype(F32) * gate * scale).astype(BF).astype(F32) for r in range(SPREAD)]
        for d in (-1, 0, 1):
            total = jnp.zeros((KINDS, BLK), F32)
            for r in range(SPREAD):
                pick = jnp.where(lat_rows[o, r] == lat * 2 + o + d, 1.0, 0.0).astype(F32)
                total = total + filt[r] * pick
            parts.append(total.astype(BF).astype(F32))
    f_lift, f_level = lift_of(jnp.concatenate(parts, axis=0))
    g_lift, g_level = lift_of(jnp.concatenate([grid_ref[0], grid_ref[1]], axis=0).astype(F32))
    parts = [part * f_lift for part in parts]
    for o, at in ((0, 1), (1, 7)):
        first, extent = windows[o, 0].astype(F32), windows[o, 1].astype(F32)
        row = jnp.where(lane == 0, first, jnp.where(lane == 1, extent, 0.0))
        row = jnp.where(lane == 2, g_level, jnp.where(lane == 3, f_level, row))
        parts.insert(at, row * (2.0**LIFT / NB))
    parts.append(jnp.zeros((FROWS - 6 * KINDS - 2, BLK), F32))
    out_ref[XROWS : XROWS + FROWS] = jnp.concatenate(parts, axis=0).astype(BF)
    mixed = jnp.concatenate([grid_ref[0, BLK:CH], grid_ref[1, BLK:CH]], axis=0)
    for n, rows in enumerate((grid_ref[0, 0:BLK], grid_ref[1, 0:BLK], mixed)):
        out_ref[n * BLK : (n + 1) * BLK] = (rows.T.astype(F32) * g_lift).astype(BF)


def window_row(ref, q, at):
    return ref[q, at : at + 16, :].astype(F32)[WINDOW_ROW : WINDOW_ROW + 1]


def any_level(tiles):
    most = functools.reduce(jnp.maximum, [tile.astype(F32) for tile in tiles])
    row = lax.broadcasted_iota(jnp.int32, most.shape, 0)
    lane = lax.broadcasted_iota(jnp.int32, most.shape, 1)
    here = (row == WINDOW_ROW) & ((lane == 2) | (lane == 3))
    return jnp.max(jnp.where(here, most, 0.0)) > 0


def lower(ref, q, at, lane):
    level = window_row(ref, q, at)[:, lane : lane + 1] * float(NB)
    scale = jnp.full((1, 1), 1.0, F32)
    for n in range(1, LEVELS):
        scale = jnp.where(level == float(n), 2.0 ** (-STEP * n), scale)
    return scale


def load_grid(xt, g_ref, start, i, lifted):
    half = CH - BLK

    def row_of_block(q):
        return pl.multiple_of(lax.rem(q - start + 2 * NB, NB) * BLK, BLK)

    for q in range(NB):
        row = row_of_block(q)
        xt[pl.ds(row, BLK), 0:BLK] = g_ref[q, i * BLK : (i + 1) * BLK, :]
        tail = g_ref[q, 2 * BLK : 3 * BLK, :]
        if i == 1:
            tail = jnp.concatenate([tail[:, half:], tail[:, :half]], axis=1)
        xt[pl.ds(row, BLK), BLK : 2 * BLK] = tail

    @pl.when(lifted)
    def _():
        @pl.loop(0, NB)
        def _(q):
            rows = pl.ds(row_of_block(q), BLK)
            xt[rows, :] = (xt[rows, :].astype(F32) * lower(g_ref, q, XROWS, 2)).astype(BF)

    xt[TOTAL : TOTAL + BLK, :] = xt[0:BLK, :]


def load_filters(fv, f_ref, at, rows, start, lifted, info):
    def lanes_of_block(q):
        return pl.ds(pl.multiple_of(lax.rem(q - start + NB, NB) * BLK, BLK), BLK)

    for q in range(NB):
        fv[0:rows, lanes_of_block(q)] = f_ref[q, at : at + rows, :].astype(F32)

    @pl.when(lifted)
    def _():
        @pl.loop(0, NB)
        def _(q):
            lanes = lanes_of_block(q)
            fv[0:rows, lanes] = fv[0:rows, lanes] * lower(f_ref, q, info, 3)


def correlate(xt, fv, s_ref, hs, before, at, slot, length):
    base = slot * KINDS * SUB
    for k in range(KINDS):
        row = fv[at + k : at + k + 1, 0:length]
        wide = jnp.broadcast_to(row, (SUB, length))
        skew = pltpu.roll(wide, 0, 1, stride=1, stride_axis=0)
        m = base + k * SUB
        s_ref[m : m + SUB, 0:length] = skew.astype(BF)
    for start in range(0, BLK, SUB):
        filters = s_ref[base : base + KINDS * SUB, 0:length]
        h = jnp.dot(filters, xt[start : start + length, :], preferred_element_type=F32)
        n = slot * BLK + start
        for k in range(KINDS):
            part = h[k * SUB : (k + 1) * SUB]
            if before is not None:
                part = part + before[k, n : n + SUB, :].astype(F32)
            hs[k, n : n + SUB, :] = part.astype(BF)


def mix(w_ref, hs):
    total = None
    for k in range(KINDS):
        part = lax.dot_general(w_ref[k], hs[k, :, 0:CH], (((0,), (1,)), ((), ())), preferred_element_type=F32)
        total = part if total is None else total + part
    return total[:, 0:BLK], total[:, BLK : 2 * BLK]


def by_width(extent, widths, run):
    below = 0
    for n, width in enumerate(widths):
        last = n == len(widths) - 1

        @pl.when((extent >= below) if last else (extent >= below) & (extent < width))
        def _(width=width):
            run(width * BLK)

        below = width


def correlate_own(i, starts, windows, g_ref, xt, fv, s_ref, hs, before):
    lon = lax.axis_index("lon")
    lifted = any_level([g_ref[q, XROWS : XROWS + 16, :] for q in range(NB)])
    dense = jnp.minimum(windows[0, 1], windows[1, 1]) >= WIDTHS[-1]

    @pl.when(dense)
    def _():
        load_grid(xt, g_ref, lon, i, lifted)
        load_filters(fv, g_ref, XROWS, FROWS, 0, lifted, XROWS)
        for o in range(2):
            correlate(xt, fv, s_ref, hs, before, starts[o], o, TOTAL)

    @pl.when(jnp.logical_not(dense))
    def _():
        for o in range(2):
            load_grid(xt, g_ref, lon + windows[o, 0], i, lifted)
            least = starts[o] // 16 * 16
            load_filters(fv, g_ref, XROWS + least, 32, windows[o, 0], lifted, XROWS)
            run = functools.partial(correlate, xt, fv, s_ref, hs, before, starts[o] - least, o)
            by_width(windows[o, 1], WIDTHS + (NB,), run)


def first_kernel(windows, g_ref, hs, xt, fv, s_ref):
    correlate_own(0, (row_of(0, 0), row_of(1, -1)), windows, g_ref, xt, fv, s_ref, hs, None)


def second_kernel(windows, g_ref, w_ref, before, out_ref, xt, fv, s_ref, hs):
    correlate_own(1, (row_of(0, 1), row_of(1, 0)), windows, g_ref, xt, fv, s_ref, hs, before)
    out_ref[0], out_ref[1] = mix(w_ref, hs)


def edge_kernel(g_ref, w_ref, fa_ref, fb_ref, a_ref, b_ref, xt, fv, s_ref, got, hs):
    lon, lat = lax.axis_index("lon"), lax.axis_index("lat")
    even = lax.rem(lat, 2) == 0
    grid_lifted = any_level([g_ref[q, XROWS : XROWS + 16, :] for q in range(NB)])
    for i in range(2):
        there = (lat > 0) if i == 0 else (lat < lax.axis_size("lat") - 1)
        take_a = jnp.logical_not(even) if i == 0 else even

        @pl.when(there)
        def _(i=i, take_a=take_a):
            tiles = [jnp.where(take_a, fa_ref[q].astype(F32), fb_ref[q].astype(F32)) for q in range(NB)]
            for q in range(NB):
                got[q] = tiles[q].astype(BF)
            ints = (tiles[0] * float(NB)).astype(jnp.int32)
            first, extent = ints[WINDOW_ROW, 0], ints[WINDOW_ROW, 1]
            load_grid(xt, g_ref, lon + first, i, grid_lifted)
            load_filters(fv, got, 0, 16, first, any_level(tiles), 0)
            by_width(extent, WIDTHS + (NB,), functools.partial(correlate, xt, fv, s_ref, hs, None, 0, i))

        @pl.when(jnp.logical_not(there))
        def _(i=i):
            hs[:, i * BLK : (i + 1) * BLK, :] = jnp.zeros((KINDS, BLK, 2 * BLK), BF)

    low, high = mix(w_ref, hs)
    a_ref[...] = jnp.where(even, high, low).astype(BF)
    b_ref[...] = jnp.where(even, low, high).astype(BF)


def prepare(windows, lat_rows, grid, psi):
    smem, vmem = pl.BlockSpec(memory_space=pltpu.SMEM), pl.BlockSpec(memory_space=pltpu.VMEM)
    return pl.pallas_call(
        prepare_kernel,
        out_shape=jax.ShapeDtypeStruct((XROWS + FROWS, BLK), BF),
        in_specs=[smem, smem, vmem, vmem],
        out_specs=vmem,
    )(windows, lat_rows, grid, psi)


def call(kernel, scalars, arrays, out_shape, frows, more=(HELD,)):
    smem, vmem = pl.BlockSpec(memory_space=pltpu.SMEM), pl.BlockSpec(memory_space=pltpu.VMEM)
    return pl.pallas_call(
        kernel,
        out_shape=out_shape,
        in_specs=[smem] * len(scalars) + [vmem] * len(arrays),
        out_specs=jax.tree.map(lambda _: vmem, out_shape),
        scratch_shapes=[
            pltpu.VMEM((TOTAL + BLK, 2 * BLK), BF),
            pltpu.VMEM((frows, TOTAL), F32),
            pltpu.VMEM((2 * KINDS * SUB, TOTAL), BF),
        ]
        + [pltpu.VMEM(shape, BF) for shape in more],
        compiler_params=pltpu.CompilerParams(vmem_limit_bytes=40 * 1024 * 1024),
        cost_estimate=pl.CostEstimate(flops=2_000_000_000, bytes_accessed=3_000_000, transcendentals=0),
    )(*scalars, *arrays)


def local(grid, psi, weight, windows, lat_rows):
    even = lax.rem(lax.axis_index("lat"), 2) == 0
    nlat = lax.axis_size("lat")
    pairs_a = [(j, j ^ 1) for j in range(nlat)]
    pairs_b = []
    for j in range(nlat):
        for n in range(NB):
            to = (j, n ^ 1) if j in (0, nlat - 1) else (j - 1 + 2 * (j % 2), n)
            pairs_b.append((j * NB + n, to[0] * NB + to[1]))

    msg = prepare(windows, lat_rows, grid, jnp.transpose(psi, (0, 2, 1, 3)))
    held = lax.all_gather(msg.astype(F16), "lon", axis=0, tiled=False)
    g = (held.astype(F32) * 2.0**-LIFT).astype(BF)

    low_at, high_at = XROWS + row_of(0, -1), XROWS + row_of(1, 1)
    low_filters, high_filters = g[:, low_at : low_at + 16], g[:, high_at : high_at + 16]
    filters_a = lax.ppermute(jnp.where(even, high_filters, low_filters), "lat", pairs_a)
    filters_b = lax.ppermute(jnp.where(even, low_filters, high_filters), ("lat", "lon"), pairs_b)

    halves = jax.ShapeDtypeStruct((2, CH, BLK), F32)
    edge = jax.ShapeDtypeStruct((CH, BLK), BF)
    first = call(first_kernel, (windows,), (g,), jax.ShapeDtypeStruct(HELD, BF), FROWS, more=())
    edge_a, edge_b = call(edge_kernel, (), (g, weight, filters_a, filters_b), (edge, edge), 16, ((NB, 16, BLK), HELD))
    got_a = lax.ppermute(edge_a, "lat", pairs_a).astype(F32)
    got_b = lax.ppermute(edge_b, ("lat", "lon"), pairs_b).astype(F32)
    both = call(second_kernel, (windows,), (g, weight, first), halves, FROWS)
    to_first, to_second = jnp.where(even, got_b, got_a), jnp.where(even, got_a, got_b)
    return jnp.stack([both[0] + to_first, both[1] + to_second]).astype(BF)


def solution(mesh):
    placed = (
        P(("ens", "lat"), None, "lon"),
        P(None, "lat", None, "lon"),
        P(),
        P("lat", None),
        P("lat", None),
    )
    return jax.shard_map(
        local, mesh=mesh, in_specs=placed, out_specs=P(("ens", "lat"), None, "lon"), check_vma=False
    )
```

```python
import functools

import jax
import jax.numpy as jnp
from jax import lax
from jax.experimental import pallas as pl
from jax.experimental.pallas import tpu as pltpu
from jax.sharding import PartitionSpec as P

BF = jnp.bfloat16
F16 = jnp.float16
F32 = jnp.float32
KINDS = 9
SPREAD = 3
CH = 192
BLK = 128
NB = 16
TOTAL = BLK * NB
SUB = 32
FROWS = 64
XROWS = 3 * BLK
LEVELS = 10
LIFT, STEP = 13, 12
WIDTHS = (4, 6, 8, 10, 12)
WINDOW_ROW = KINDS
HELD = (KINDS, 2 * BLK, 2 * BLK)


def row_of(o, d):
    return (o * 3 + d + 1) * KINDS + (1 if (o, d) != (0, -1) else 0)


def lift_of(values):
    most = jnp.max(jnp.max(jnp.abs(values), axis=0, keepdims=True), axis=1, keepdims=True)
    lift = jnp.full((1, 1), 2.0**LIFT, F32)
    level = jnp.zeros((1, 1), F32)
    for n in range(1, LEVELS):
        small = (most < 2.0 ** (3 - STEP * n)) & (most > 0.0)
        lift = jnp.where(small, 2.0 ** (LIFT + STEP * n), lift)
        level = jnp.where(small, float(n), level)
    return lift, level


def prepare_kernel(windows, lat_rows, grid_ref, psi_ref, out_ref):
    lon, lat = lax.axis_index("lon"), lax.axis_index("lat")
    lane = lax.broadcasted_iota(jnp.int32, (1, BLK), 1)
    parts = []
    for o in range(2):
        first, extent = windows[o, 0], windows[o, 1]
        inside = lax.rem(lon - first + NB, NB) < extent
        scale = lax.rsqrt(jnp.full((1, BLK), extent, jnp.int32).astype(F32) * float(KINDS * SPREAD * BLK))
        gate = jnp.where(inside, 1.0, 0.0).astype(F32)
        filt = [(psi_ref[:, r, o, :].astype(F32) * gate * scale).astype(BF).astype(F32) for r in range(SPREAD)]
        for d in (-1, 0, 1):
            total = jnp.zeros((KINDS, BLK), F32)
            for r in range(SPREAD):
                pick = jnp.where(lat_rows[o, r] == lat * 2 + o + d, 1.0, 0.0).astype(F32)
                total = total + filt[r] * pick
            parts.append(total.astype(BF).astype(F32))
    f_lift, f_level = lift_of(jnp.concatenate(parts, axis=0))
    g_lift, g_level = lift_of(jnp.concatenate([grid_ref[0], grid_ref[1]], axis=0).astype(F32))
    parts = [part * f_lift for part in parts]
    for o, at in ((0, 1), (1, 7)):
        first, extent = windows[o, 0].astype(F32), windows[o, 1].astype(F32)
        row = jnp.where(lane == 0, first, jnp.where(lane == 1, extent, 0.0))
        row = jnp.where(lane == 2, g_level, jnp.where(lane == 3, f_level, row))
        parts.insert(at, row * (2.0**LIFT / NB))
    parts.append(jnp.zeros((FROWS - 6 * KINDS - 2, BLK), F32))
    out_ref[XROWS : XROWS + FROWS] = jnp.concatenate(parts, axis=0).astype(BF)
    mixed = jnp.concatenate([grid_ref[0, BLK:CH], grid_ref[1, BLK:CH]], axis=0)
    for n, rows in enumerate((grid_ref[0, 0:BLK], grid_ref[1, 0:BLK], mixed)):
        out_ref[n * BLK : (n + 1) * BLK] = (rows.T.astype(F32) * g_lift).astype(BF)


def window_row(ref, q, at):
    return ref[q, at : at + 16, :].astype(F32)[WINDOW_ROW : WINDOW_ROW + 1]


def any_level(tiles):
    most = functools.reduce(jnp.maximum, [tile.astype(F32) for tile in tiles])
    row = lax.broadcasted_iota(jnp.int32, most.shape, 0)
    lane = lax.broadcasted_iota(jnp.int32, most.shape, 1)
    here = (row == WINDOW_ROW) & ((lane == 2) | (lane == 3))
    return jnp.max(jnp.where(here, most, 0.0)) > 0


def lower(ref, q, at, lane):
    level = window_row(ref, q, at)[:, lane : lane + 1] * float(NB)
    scale = jnp.full((1, 1), 1.0, F32)
    for n in range(1, LEVELS):
        scale = jnp.where(level == float(n), 2.0 ** (-STEP * n), scale)
    return scale


def load_grid(xt, g_ref, start, i, lifted):
    half = CH - BLK

    def row_of_block(q):
        return pl.multiple_of(lax.rem(q - start + 2 * NB, NB) * BLK, BLK)

    for q in range(NB):
        row = row_of_block(q)
        xt[pl.ds(row, BLK), 0:BLK] = g_ref[q, i * BLK : (i + 1) * BLK, :]
        tail = g_ref[q, 2 * BLK : 3 * BLK, :]
        if i == 1:
            tail = jnp.concatenate([tail[:, half:], tail[:, :half]], axis=1)
        xt[pl.ds(row, BLK), BLK : 2 * BLK] = tail

    @pl.when(lifted)
    def _():
        @pl.loop(0, NB)
        def _(q):
            rows = pl.ds(row_of_block(q), BLK)
            xt[rows, :] = (xt[rows, :].astype(F32) * lower(g_ref, q, XROWS, 2)).astype(BF)

    xt[TOTAL : TOTAL + BLK, :] = xt[0:BLK, :]


def load_filters(fv, f_ref, at, rows, start, lifted, info):
    def lanes_of_block(q):
        return pl.ds(pl.multiple_of(lax.rem(q - start + NB, NB) * BLK, BLK), BLK)

    for q in range(NB):
        fv[0:rows, lanes_of_block(q)] = f_ref[q, at : at + rows, :].astype(F32)

    @pl.when(lifted)
    def _():
        @pl.loop(0, NB)
        def _(q):
            lanes = lanes_of_block(q)
            fv[0:rows, lanes] = fv[0:rows, lanes] * lower(f_ref, q, info, 3)


def correlate(xt, fv, s_ref, hs, before, at, slot, length):
    base = slot * KINDS * SUB
    for k in range(KINDS):
        row = fv[at + k : at + k + 1, 0:length]
        wide = jnp.broadcast_to(row, (SUB, length))
        skew = pltpu.roll(wide, 0, 1, stride=1, stride_axis=0)
        m = base + k * SUB
        s_ref[m : m + SUB, 0:length] = skew.astype(BF)
    for start in range(0, BLK, SUB):
        filters = s_ref[base : base + KINDS * SUB, 0:length]
        h = jnp.dot(filters, xt[start : start + length, :], preferred_element_type=F32)
        n = slot * BLK + start
        for k in range(KINDS):
            part = h[k * SUB : (k + 1) * SUB]
            if before is not None:
                part = part + before[k, n : n + SUB, :].astype(F32)
            hs[k, n : n + SUB, :] = part.astype(BF)


def mix(w_ref, hs):
    total = None
    for k in range(KINDS):
        part = lax.dot_general(w_ref[k], hs[k, :, 0:CH], (((0,), (1,)), ((), ())), preferred_element_type=F32)
        total = part if total is None else total + part
    return total[:, 0:BLK], total[:, BLK : 2 * BLK]


def by_width(extent, widths, run):
    below = 0
    for n, width in enumerate(widths):
        last = n == len(widths) - 1

        @pl.when((extent >= below) if last else (extent >= below) & (extent < width))
        def _(width=width):
            run(width * BLK)

        below = width


def correlate_own(i, starts, windows, g_ref, xt, fv, s_ref, hs, before):
    lon = lax.axis_index("lon")
    lifted = any_level([g_ref[q, XROWS : XROWS + 16, :] for q in range(NB)])
    dense = jnp.minimum(windows[0, 1], windows[1, 1]) >= WIDTHS[-1]

    @pl.when(dense)
    def _():
        load_grid(xt, g_ref, lon, i, lifted)
        load_filters(fv, g_ref, XROWS, FROWS, 0, lifted, XROWS)
        for o in range(2):
            correlate(xt, fv, s_ref, hs, before, starts[o], o, TOTAL)

    @pl.when(jnp.logical_not(dense))
    def _():
        for o in range(2):
            load_grid(xt, g_ref, lon + windows[o, 0], i, lifted)
            least = starts[o] // 16 * 16
            load_filters(fv, g_ref, XROWS + least, 32, windows[o, 0], lifted, XROWS)
            run = functools.partial(correlate, xt, fv, s_ref, hs, before, starts[o] - least, o)
            by_width(windows[o, 1], WIDTHS + (NB,), run)


def first_kernel(windows, g_ref, hs, xt, fv, s_ref):
    correlate_own(0, (row_of(0, 0), row_of(1, -1)), windows, g_ref, xt, fv, s_ref, hs, None)


def second_kernel(windows, g_ref, w_ref, before, out_ref, xt, fv, s_ref, hs):
    correlate_own(1, (row_of(0, 1), row_of(1, 0)), windows, g_ref, xt, fv, s_ref, hs, before)
    out_ref[0], out_ref[1] = mix(w_ref, hs)


def edge_kernel(g_ref, w_ref, fa_ref, fb_ref, a_ref, b_ref, xt, fv, s_ref, got, hs):
    lon, lat = lax.axis_index("lon"), lax.axis_index("lat")
    even = lax.rem(lat, 2) == 0
    grid_lifted = any_level([g_ref[q, XROWS : XROWS + 16, :] for q in range(NB)])
    for i in range(2):
        there = (lat > 0) if i == 0 else (lat < lax.axis_size("lat") - 1)
        take_a = jnp.logical_not(even) if i == 0 else even

        @pl.when(there)
        def _(i=i, take_a=take_a):
            tiles = [jnp.where(take_a, fa_ref[q].astype(F32), fb_ref[q].astype(F32)) for q in range(NB)]
            for q in range(NB):
                got[q] = tiles[q].astype(BF)
            ints = (tiles[0] * float(NB)).astype(jnp.int32)
            first, extent = ints[WINDOW_ROW, 0], ints[WINDOW_ROW, 1]
            load_grid(xt, g_ref, lon + first, i, grid_lifted)
            load_filters(fv, got, 0, 16, first, any_level(tiles), 0)
            by_width(extent, WIDTHS + (NB,), functools.partial(correlate, xt, fv, s_ref, hs, None, 0, i))

        @pl.when(jnp.logical_not(there))
        def _(i=i):
            hs[:, i * BLK : (i + 1) * BLK, :] = jnp.zeros((KINDS, BLK, 2 * BLK), BF)

    low, high = mix(w_ref, hs)
    a_ref[...] = jnp.where(even, high, low).astype(BF)
    b_ref[...] = jnp.where(even, low, high).astype(BF)


def prepare(windows, lat_rows, grid, psi):
    smem, vmem = pl.BlockSpec(memory_space=pltpu.SMEM), pl.BlockSpec(memory_space=pltpu.VMEM)
    return pl.pallas_call(
        prepare_kernel,
        out_shape=jax.ShapeDtypeStruct((XROWS + FROWS, BLK), BF),
        in_specs=[smem, smem, vmem, vmem],
        out_specs=vmem,
    )(windows, lat_rows, grid, psi)


def call(kernel, scalars, arrays, out_shape, frows, more=(HELD,)):
    smem, vmem = pl.BlockSpec(memory_space=pltpu.SMEM), pl.BlockSpec(memory_space=pltpu.VMEM)
    return pl.pallas_call(
        kernel,
        out_shape=out_shape,
        in_specs=[smem] * len(scalars) + [vmem] * len(arrays),
        out_specs=jax.tree.map(lambda _: vmem, out_shape),
        scratch_shapes=[
            pltpu.VMEM((TOTAL + BLK, 2 * BLK), BF),
            pltpu.VMEM((frows, TOTAL), F32),
            pltpu.VMEM((2 * KINDS * SUB, TOTAL), BF),
        ]
        + [pltpu.VMEM(shape, BF) for shape in more],
        compiler_params=pltpu.CompilerParams(vmem_limit_bytes=40 * 1024 * 1024),
        cost_estimate=pl.CostEstimate(flops=2_000_000_000, bytes_accessed=3_000_000, transcendentals=0),
    )(*scalars, *arrays)


def local(grid, psi, weight, windows, lat_rows):
    even = lax.rem(lax.axis_index("lat"), 2) == 0
    nlat = lax.axis_size("lat")
    pairs_a = [(j, j ^ 1) for j in range(nlat)]
    pairs_b = []
    for j in range(nlat):
        for n in range(NB):
            to = (j, n ^ 1) if j in (0, nlat - 1) else (j - 1 + 2 * (j % 2), n)
            pairs_b.append((j * NB + n, to[0] * NB + to[1]))

    msg = prepare(windows, lat_rows, grid, jnp.transpose(psi, (0, 2, 1, 3)))
    held = lax.all_gather(msg.astype(F16), "lon", axis=0, tiled=False)
    g = (held.astype(F32) * 2.0**-LIFT).astype(BF)

    low_at, high_at = XROWS + row_of(0, -1), XROWS + row_of(1, 1)
    low_filters, high_filters = g[:, low_at : low_at + 16], g[:, high_at : high_at + 16]
    filters_a = lax.ppermute(jnp.where(even, high_filters, low_filters), "lat", pairs_a)
    filters_b = lax.ppermute(jnp.where(even, low_filters, high_filters), ("lat", "lon"), pairs_b)

    halves = jax.ShapeDtypeStruct((2, CH, BLK), F32)
    edge = jax.ShapeDtypeStruct((CH, BLK), BF)
    first = call(first_kernel, (windows,), (g,), jax.ShapeDtypeStruct(HELD, BF), FROWS, more=())
    edge_a, edge_b = call(edge_kernel, (), (g, weight, filters_a, filters_b), (edge, edge), 16, ((NB, 16, BLK), HELD))
    got_a = lax.ppermute(edge_a, "lat", pairs_a).astype(F32)
    got_b = lax.ppermute(edge_b, ("lat", "lon"), pairs_b).astype(F32)
    both = call(second_kernel, (windows,), (g, weight, first), halves, FROWS)
    to_first, to_second = jnp.where(even, got_b, got_a), jnp.where(even, got_a, got_b)
    return jnp.stack([both[0] + to_first, both[1] + to_second]).astype(BF)


def solution(mesh):
    placed = (
        P(("ens", "lat"), None, "lon"),
        P(None, "lat", None, "lon"),
        P(),
        P("lat", None),
        P("lat", None),
    )
    return jax.shard_map(
        local, mesh=mesh, in_specs=placed, out_specs=P(("ens", "lat"), None, "lon"), check_vma=False
    )
```

```python
import functools

import jax
import jax.numpy as jnp
from jax import lax
from jax.experimental import pallas as pl
from jax.experimental.pallas import tpu as pltpu
from jax.sharding import PartitionSpec as P

BF = jnp.bfloat16
F16 = jnp.float16
F32 = jnp.float32
KINDS = 9
SPREAD = 3
CH = 192
BLK = 128
NB = 16
TOTAL = BLK * NB
SUB = 16
FROWS = 64
XROWS = 3 * BLK
LEVELS = 10
LIFT, STEP = 13, 12
WIDTHS = (4, 8, 12)
WINDOW_ROW = KINDS
HELD = (KINDS, 2 * BLK, 2 * BLK)


def row_of(o, d):
    return (o * 3 + d + 1) * KINDS + (1 if (o, d) != (0, -1) else 0)


def lift_of(values):
    most = jnp.max(jnp.max(jnp.abs(values), axis=0, keepdims=True), axis=1, keepdims=True)
    lift = jnp.full((1, 1), 2.0**LIFT, F32)
    level = jnp.zeros((1, 1), F32)
    for n in range(1, LEVELS):
        small = (most < 2.0 ** (3 - STEP * n)) & (most > 0.0)
        lift = jnp.where(small, 2.0 ** (LIFT + STEP * n), lift)
        level = jnp.where(small, float(n), level)
    return lift, level


def prepare_kernel(windows, lat_rows, grid_ref, psi_ref, out_ref):
    lon, lat = lax.axis_index("lon"), lax.axis_index("lat")
    lane = lax.broadcasted_iota(jnp.int32, (1, BLK), 1)
    parts = []
    for o in range(2):
        first, extent = windows[o, 0], windows[o, 1]
        inside = lax.rem(lon - first + NB, NB) < extent
        scale = lax.rsqrt(jnp.full((1, BLK), extent, jnp.int32).astype(F32) * float(KINDS * SPREAD * BLK))
        gate = jnp.where(inside, 1.0, 0.0).astype(F32)
        filt = [(psi_ref[:, r, o, :].astype(F32) * gate * scale).astype(BF).astype(F32) for r in range(SPREAD)]
        for d in (-1, 0, 1):
            total = jnp.zeros((KINDS, BLK), F32)
            for r in range(SPREAD):
                pick = jnp.where(lat_rows[o, r] == lat * 2 + o + d, 1.0, 0.0).astype(F32)
                total = total + filt[r] * pick
            parts.append(total.astype(BF).astype(F32))
    f_lift, f_level = lift_of(jnp.concatenate(parts, axis=0))
    g_lift, g_level = lift_of(jnp.concatenate([grid_ref[0], grid_ref[1]], axis=0).astype(F32))
    parts = [part * f_lift for part in parts]
    for o, at in ((0, 1), (1, 7)):
        first, extent = windows[o, 0].astype(F32), windows[o, 1].astype(F32)
        row = jnp.where(lane == 0, first, jnp.where(lane == 1, extent, 0.0))
        row = jnp.where(lane == 2, g_level, jnp.where(lane == 3, f_level, row))
        parts.insert(at, row * (2.0**LIFT / NB))
    parts.append(jnp.zeros((FROWS - 6 * KINDS - 2, BLK), F32))
    out_ref[XROWS : XROWS + FROWS] = jnp.concatenate(parts, axis=0).astype(BF)
    mixed = jnp.concatenate([grid_ref[0, BLK:CH], grid_ref[1, BLK:CH]], axis=0)
    for n, rows in enumerate((grid_ref[0, 0:BLK], grid_ref[1, 0:BLK], mixed)):
        out_ref[n * BLK : (n + 1) * BLK] = (rows.T.astype(F32) * g_lift).astype(BF)


def window_row(ref, q, at):
    return ref[q, at : at + 16, :].astype(F32)[WINDOW_ROW : WINDOW_ROW + 1]


def any_level(tiles):
    most = functools.reduce(jnp.maximum, [tile.astype(F32) for tile in tiles])
    row = lax.broadcasted_iota(jnp.int32, most.shape, 0)
    lane = lax.broadcasted_iota(jnp.int32, most.shape, 1)
    here = (row == WINDOW_ROW) & ((lane == 2) | (lane == 3))
    return jnp.max(jnp.where(here, most, 0.0)) > 0


def lower(ref, q, at, lane):
    level = window_row(ref, q, at)[:, lane : lane + 1] * float(NB)
    scale = jnp.full((1, 1), 1.0, F32)
    for n in range(1, LEVELS):
        scale = jnp.where(level == float(n), 2.0 ** (-STEP * n), scale)
    return scale


def load_grid(xt, g_ref, start, i, lifted):
    half = CH - BLK

    def row_of_block(q):
        return pl.multiple_of(lax.rem(q - start + 2 * NB, NB) * BLK, BLK)

    for q in range(NB):
        row = row_of_block(q)
        xt[pl.ds(row, BLK), 0:BLK] = g_ref[q, i * BLK : (i + 1) * BLK, :]
        tail = g_ref[q, 2 * BLK : 3 * BLK, :]
        if i == 1:
            tail = jnp.concatenate([tail[:, half:], tail[:, :half]], axis=1)
        xt[pl.ds(row, BLK), BLK : 2 * BLK] = tail

    @pl.when(lifted)
    def _():
        @pl.loop(0, NB)
        def _(q):
            rows = pl.ds(row_of_block(q), BLK)
            xt[rows, :] = (xt[rows, :].astype(F32) * lower(g_ref, q, XROWS, 2)).astype(BF)

    xt[TOTAL : TOTAL + BLK, :] = xt[0:BLK, :]


def load_filters(fv, f_ref, at, rows, start, lifted, info):
    def lanes_of_block(q):
        return pl.ds(pl.multiple_of(lax.rem(q - start + NB, NB) * BLK, BLK), BLK)

    for q in range(NB):
        fv[0:rows, lanes_of_block(q)] = f_ref[q, at : at + rows, :].astype(F32)

    @pl.when(lifted)
    def _():
        @pl.loop(0, NB)
        def _(q):
            lanes = lanes_of_block(q)
            fv[0:rows, lanes] = fv[0:rows, lanes] * lower(f_ref, q, info, 3)


def correlate(xt, fv, s_ref, hs, before, at, slot, length):
    base = slot * KINDS * SUB
    for k in range(KINDS):
        row = fv[at + k : at + k + 1, 0:length]
        wide = jnp.broadcast_to(row, (SUB, length))
        skew = pltpu.roll(wide, 0, 1, stride=1, stride_axis=0)
        m = base + k * SUB
        s_ref[m : m + SUB, 0:length] = skew.astype(BF)
    for start in range(0, BLK, SUB):
        filters = s_ref[base : base + KINDS * SUB, 0:length]
        h = jnp.dot(filters, xt[start : start + length, :], preferred_element_type=F32)
        n = slot * BLK + start
        for k in range(KINDS):
            part = h[k * SUB : (k + 1) * SUB]
            if before is not None:
                part = part + before[k, n : n + SUB, :].astype(F32)
            hs[k, n : n + SUB, :] = part.astype(BF)


def mix(w_ref, hs):
    total = None
    for k in range(KINDS):
        part = lax.dot_general(w_ref[k], hs[k, :, 0:CH], (((0,), (1,)), ((), ())), preferred_element_type=F32)
        total = part if total is None else total + part
    return total[:, 0:BLK], total[:, BLK : 2 * BLK]


def by_width(extent, widths, run):
    below = 0
    for n, width in enumerate(widths):
        last = n == len(widths) - 1

        @pl.when((extent >= below) if last else (extent >= below) & (extent < width))
        def _(width=width):
            run(width * BLK)

        below = width


def correlate_own(i, starts, windows, g_ref, xt, fv, s_ref, hs, before):
    lon = lax.axis_index("lon")
    lifted = any_level([g_ref[q, XROWS : XROWS + 16, :] for q in range(NB)])
    dense = jnp.minimum(windows[0, 1], windows[1, 1]) >= WIDTHS[-1]

    @pl.when(dense)
    def _():
        load_grid(xt, g_ref, lon, i, lifted)
        load_filters(fv, g_ref, XROWS, FROWS, 0, lifted, XROWS)
        for o in range(2):
            correlate(xt, fv, s_ref, hs, before, starts[o], o, TOTAL)

    @pl.when(jnp.logical_not(dense))
    def _():
        for o in range(2):
            load_grid(xt, g_ref, lon + windows[o, 0], i, lifted)
            least = starts[o] // 16 * 16
            load_filters(fv, g_ref, XROWS + least, 32, windows[o, 0], lifted, XROWS)
            run = functools.partial(correlate, xt, fv, s_ref, hs, before, starts[o] - least, o)
            by_width(windows[o, 1], WIDTHS + (NB,), run)


def first_kernel(windows, g_ref, hs, xt, fv, s_ref):
    correlate_own(0, (row_of(0, 0), row_of(1, -1)), windows, g_ref, xt, fv, s_ref, hs, None)


def second_kernel(windows, g_ref, w_ref, before, out_ref, xt, fv, s_ref, hs):
    correlate_own(1, (row_of(0, 1), row_of(1, 0)), windows, g_ref, xt, fv, s_ref, hs, before)
    out_ref[0], out_ref[1] = mix(w_ref, hs)


def edge_kernel(g_ref, w_ref, fa_ref, fb_ref, a_ref, b_ref, xt, fv, s_ref, got, hs):
    lon, lat = lax.axis_index("lon"), lax.axis_index("lat")
    even = lax.rem(lat, 2) == 0
    grid_lifted = any_level([g_ref[q, XROWS : XROWS + 16, :] for q in range(NB)])
    for i in range(2):
        there = (lat > 0) if i == 0 else (lat < lax.axis_size("lat") - 1)
        take_a = jnp.logical_not(even) if i == 0 else even

        @pl.when(there)
        def _(i=i, take_a=take_a):
            tiles = [jnp.where(take_a, fa_ref[q].astype(F32), fb_ref[q].astype(F32)) for q in range(NB)]
            for q in range(NB):
                got[q] = tiles[q].astype(BF)
            ints = (tiles[0] * float(NB)).astype(jnp.int32)
            first, extent = ints[WINDOW_ROW, 0], ints[WINDOW_ROW, 1]
            load_grid(xt, g_ref, lon + first, i, grid_lifted)
            load_filters(fv, got, 0, 16, first, any_level(tiles), 0)
            by_width(extent, WIDTHS + (NB,), functools.partial(correlate, xt, fv, s_ref, hs, None, 0, i))

        @pl.when(jnp.logical_not(there))
        def _(i=i):
            hs[:, i * BLK : (i + 1) * BLK, :] = jnp.zeros((KINDS, BLK, 2 * BLK), BF)

    low, high = mix(w_ref, hs)
    a_ref[...] = jnp.where(even, high, low).astype(BF)
    b_ref[...] = jnp.where(even, low, high).astype(BF)


def prepare(windows, lat_rows, grid, psi):
    smem, vmem = pl.BlockSpec(memory_space=pltpu.SMEM), pl.BlockSpec(memory_space=pltpu.VMEM)
    return pl.pallas_call(
        prepare_kernel,
        out_shape=jax.ShapeDtypeStruct((XROWS + FROWS, BLK), BF),
        in_specs=[smem, smem, vmem, vmem],
        out_specs=vmem,
    )(windows, lat_rows, grid, psi)


def call(kernel, scalars, arrays, out_shape, frows, more=(HELD,)):
    smem, vmem = pl.BlockSpec(memory_space=pltpu.SMEM), pl.BlockSpec(memory_space=pltpu.VMEM)
    return pl.pallas_call(
        kernel,
        out_shape=out_shape,
        in_specs=[smem] * len(scalars) + [vmem] * len(arrays),
        out_specs=jax.tree.map(lambda _: vmem, out_shape),
        scratch_shapes=[
            pltpu.VMEM((TOTAL + BLK, 2 * BLK), BF),
            pltpu.VMEM((frows, TOTAL), F32),
            pltpu.VMEM((2 * KINDS * SUB, TOTAL), BF),
        ]
        + [pltpu.VMEM(shape, BF) for shape in more],
        compiler_params=pltpu.CompilerParams(vmem_limit_bytes=40 * 1024 * 1024),
        cost_estimate=pl.CostEstimate(flops=2_000_000_000, bytes_accessed=3_000_000, transcendentals=0),
    )(*scalars, *arrays)


def local(grid, psi, weight, windows, lat_rows):
    even = lax.rem(lax.axis_index("lat"), 2) == 0
    nlat = lax.axis_size("lat")
    pairs_a = [(j, j ^ 1) for j in range(nlat)]
    pairs_b = []
    for j in range(nlat):
        for n in range(NB):
            to = (j, n ^ 1) if j in (0, nlat - 1) else (j - 1 + 2 * (j % 2), n)
            pairs_b.append((j * NB + n, to[0] * NB + to[1]))

    msg = prepare(windows, lat_rows, grid, jnp.transpose(psi, (0, 2, 1, 3)))
    held = lax.all_gather(msg.astype(F16), "lon", axis=0, tiled=False)
    g = (held.astype(F32) * 2.0**-LIFT).astype(BF)

    low_at, high_at = XROWS + row_of(0, -1), XROWS + row_of(1, 1)
    low_filters, high_filters = g[:, low_at : low_at + 16], g[:, high_at : high_at + 16]
    filters_a = lax.ppermute(jnp.where(even, high_filters, low_filters), "lat", pairs_a)
    filters_b = lax.ppermute(jnp.where(even, low_filters, high_filters), ("lat", "lon"), pairs_b)

    halves = jax.ShapeDtypeStruct((2, CH, BLK), F32)
    edge = jax.ShapeDtypeStruct((CH, BLK), BF)
    first = call(first_kernel, (windows,), (g,), jax.ShapeDtypeStruct(HELD, BF), FROWS, more=())
    edge_a, edge_b = call(edge_kernel, (), (g, weight, filters_a, filters_b), (edge, edge), 16, ((NB, 16, BLK), HELD))
    got_a = lax.ppermute(edge_a, "lat", pairs_a).astype(F32)
    got_b = lax.ppermute(edge_b, ("lat", "lon"), pairs_b).astype(F32)
    both = call(second_kernel, (windows,), (g, weight, first), halves, FROWS)
    to_first, to_second = jnp.where(even, got_b, got_a), jnp.where(even, got_a, got_b)
    return jnp.stack([both[0] + to_first, both[1] + to_second]).astype(BF)


def solution(mesh):
    placed = (
        P(("ens", "lat"), None, "lon"),
        P(None, "lat", None, "lon"),
        P(),
        P("lat", None),
        P("lat", None),
    )
    return jax.shard_map(
        local, mesh=mesh, in_specs=placed, out_specs=P(("ens", "lat"), None, "lon"), check_vma=False
    )
```
